256 devices in a mesh: replica: 16 (over z_hi, x), fsdp: 16 (over y, z_lo, core).
Axes of the slice: x: 4, y: 4, z: 8 (z_hi: 4, z_lo: 2; z = z_hi * 2 + z_lo), core: 2. Of those that a mesh axis runs over, the one named last changes fastest.
Arguments:
- outer_params: float32 [384, 3072], P('fsdp'), may hold values from -4 to 4
- outer_momentum: float32 [384, 3072], P('fsdp'), may hold values from -1.5 to 1.5
- inner_mean: float32 [16, 384, 3072], P('replica', 'fsdp')
- inner_square: float32 [16, 384, 3072], P('replica', 'fsdp'), as said below
- latents: bfloat16 [2, 131072, 64], P(None, ('replica', 'fsdp')), may hold values from -6 to 6
- noise_draw: bfloat16 [2, 131072, 64], P(None, ('replica', 'fsdp')), may hold values from -6 to 6
- timesteps: int32 [2, 131072], P(None, ('replica', 'fsdp')), may hold values from 0 to 999
- fragment: int32 [1], replicated, may hold values from 0 to 14
- modulation: float32 [15, 2, 3072], replicated, may hold values from -3 to 3
Outputs:
- new_params: float32 [384, 3072], P('fsdp')
- new_momentum: float32 [384, 3072], P('fsdp')
- new_mean: float32 [16, 384, 3072], P('replica', 'fsdp')
- new_square: float32 [16, 384, 3072], P('replica', 'fsdp')
The draws below stay inside these ranges and needn't reach their ends.
Inputs may be any that keep to these rules, and one draw needn't show every extreme that they name: `inner_square`: positive.
All inputs are finite; a program needn't handle non-finite values.
Results may differ from the reference program's by a relative error of at most 0.034.
Values may be sent and summed in bfloat16 or wider, within the bound.
No kernel may reach another device: no remote copies, remote signals or barrier semaphores. Data moves between devices by JAX's collectives and lax.ppermute only.
A program may use at most 64 MiB of HBM per device.

```python
import math
import jax
import jax.numpy as jnp
from jax import lax

D = 3072
CH = 64
TEMB = 256
TOK_DEV = 512
STEPS = 2
LEVELS = 1000
NFRAG = 15
FRAG_ROWS = 384
TOKENS = 131072
N_REPLICA = 16
N_FSDP = 16


def base_square(key):
    spread = jax.random.uniform(key, (N_REPLICA, FRAG_ROWS, D), jnp.float32)
    row_index = jnp.arange(FRAG_ROWS)[None, :, None]
    time_rows = (row_index >= CH) & (row_index < CH + TEMB)
    row_factor = jnp.where(time_rows, 0.2 * CH / TEMB, 1.0).astype(jnp.float32)
    reference_level = 3.0 / (float(CH) * CH * D * TOK_DEV * N_FSDP)
    return reference_level * row_factor * jnp.exp(math.log(0.02) + spread * math.log(100.0))


def draw_inner_square(key, part):
    square = base_square(key)
    return square


def draw_inner_mean(key, part):
    square = base_square(key)
    key = jax.random.fold_in(key, 5)
    ratio = 0.5 * jax.random.normal(key, square.shape, jnp.float32)
    return jnp.sqrt(square) * ratio


def plant(values, rng, smallest, top_value):
    extent = values.shape
    index_at = [jax.random.randint(jax.random.fold_in(rng, axis), (), 0, extent[axis]) for axis in range(len(extent))]
    values = values.at[tuple(index_at)].set(smallest)
    longest = extent.index(max(extent))
    index_at[longest] = (index_at[longest] + 1) % extent[longest]
    return values.at[tuple(index_at)].set(top_value)


def block_levels(stream_key, dims, pieces, low, high):
    level = 1.0
    for position, parts in pieces:
        heights = jax.random.uniform(jax.random.fold_in(jax.random.fold_in(stream_key, 6), position), (parts,), jnp.float32, low / len(pieces), high / len(pieces))
        level = level * jnp.repeat(jnp.exp(heights), dims[position] // parts).reshape((-1,) + (1,) * (len(dims) - 1 - position))
    return level


def scatter_about(own_key, shape, scale, bound, pieces=(), kind=jnp.bfloat16):
    result = jax.random.normal(own_key, shape, jnp.float32) * scale
    if len(pieces) > 0:
        result = block_levels(own_key, shape, pieces, -0.22, 0.18) * result
    return jnp.clip(result, min=-bound, max=bound).astype(kind)


def setup_inputs(seed: int = 0) -> dict:
    splits = jax.random.split(jax.random.key(seed), 10)
    return {
        "outer_params": scatter_about(splits[0], (FRAG_ROWS, D), 0.5, 4.0, ((0, 16),), jnp.float32),
        "outer_momentum": scatter_about(splits[1], (FRAG_ROWS, D), 0.1, 1.5, ((0, 16),), jnp.float32),
        "inner_mean": draw_inner_mean(jax.random.fold_in(splits[9], 71), 0),
        "inner_square": draw_inner_square(jax.random.fold_in(splits[9], 71), 0),
        "latents": scatter_about(splits[4], (STEPS, TOKENS, CH), 1.0, 6.0, ((1, 256),)),
        "noise_draw": scatter_about(splits[5], (STEPS, TOKENS, CH), 1.0, 6.0, ((1, 256),)),
        "timesteps": plant(jax.random.randint(splits[6], (STEPS, TOKENS), 0, LEVELS), jax.random.fold_in(splits[6], 1), 0, LEVELS - 1).astype(jnp.int32),
        "fragment": jax.random.randint(splits[7], (1,), 0, NFRAG).astype(jnp.int32),
        "modulation": scatter_about(splits[8], (NFRAG, 2, D), 0.5, 3.0, (), jnp.float32),
    }


BETA_ONE = 0.9
BETA_TWO = 0.95
INNER_RATE = 0.2
DECAY_RATE = 0.1
ADAM_EPS = 1e-08
NORM_EPS = 1e-06
OUTER_RATE = 0.7
NESTEROV = 0.9

def embed_levels(levels, time_width):
    half_width = time_width // 2
    noise_level = (levels.astype(jnp.float32) + 0.5) / LEVELS
    frequencies = jnp.exp(-math.log(10000.0) * jnp.arange(half_width, dtype=jnp.float32) / half_width)
    angles = (1000.0 * noise_level)[:, None] * frequencies[None, :]
    return (jnp.concatenate([jnp.cos(angles), jnp.sin(angles)], axis=-1), noise_level)

def local_grads(weights, latent_rows, noise_rows, levels, mod_shift, mod_scale, total_rows):
    channels = latent_rows.shape[1]
    model_width = weights.shape[1]
    time_width = weights.shape[0] - 2 * channels
    in_weight = weights[:channels]
    time_weight = weights[channels:channels + time_width]
    out_weight = weights[channels + time_width:]
    level_embed, noise_level = embed_levels(levels, time_width)
    latent_f = latent_rows.astype(jnp.float32)
    noise_f = noise_rows.astype(jnp.float32)
    noised = ((1.0 - noise_level)[:, None] * latent_f + noise_level[:, None] * noise_f).astype(jnp.bfloat16)
    target = noise_f - latent_f
    embed_b = level_embed.astype(jnp.bfloat16)
    time_pre = jnp.dot(embed_b, time_weight, preferred_element_type=jnp.float32) / math.sqrt(time_width)
    hidden = jnp.dot(noised, in_weight, preferred_element_type=jnp.float32) / math.sqrt(channels) + jax.nn.silu(time_pre)
    inverse = lax.rsqrt(lax.optimization_barrier(jnp.mean(hidden * hidden, axis=-1, keepdims=True)) + NORM_EPS)
    normed = hidden * inverse
    factor = 1.0 + mod_scale
    modded = (normed * factor + mod_shift).astype(jnp.bfloat16)
    output = lax.dot_general(modded, out_weight, (((1,), (1,)), ((), ())), preferred_element_type=jnp.float32) / math.sqrt(model_width)
    out_grad = (2.0 / (total_rows * channels) * (output - target)).astype(jnp.bfloat16)
    grad_out = lax.dot_general(out_grad, modded, (((0,), (0,)), ((), ())), preferred_element_type=jnp.float32) / math.sqrt(model_width)
    mod_grad = jnp.dot(out_grad, out_weight, preferred_element_type=jnp.float32) / math.sqrt(model_width)
    norm_grad = mod_grad * factor
    hid_grad = inverse * (norm_grad - normed * lax.optimization_barrier(jnp.mean(norm_grad * normed, axis=-1, keepdims=True)))
    sigmoid_pre = jax.nn.sigmoid(time_pre)
    pre_grad = hid_grad * (sigmoid_pre * (1.0 + time_pre * (1.0 - sigmoid_pre)))
    grad_in = lax.dot_general(noised, hid_grad.astype(jnp.bfloat16), (((0,), (0,)), ((), ())), preferred_element_type=jnp.float32) / math.sqrt(channels)
    grad_time = lax.dot_general(embed_b, pre_grad.astype(jnp.bfloat16), (((0,), (0,)), ((), ())), preferred_element_type=jnp.float32) / math.sqrt(time_width)
    return jnp.concatenate([grad_in, grad_time, grad_out], axis=0)

def adam_update(params, moment_one, moment_two, gradient):
    moment_one = BETA_ONE * moment_one + (1.0 - BETA_ONE) * gradient
    moment_two = BETA_TWO * moment_two + (1.0 - BETA_TWO) * gradient * gradient
    params = params - INNER_RATE * (moment_one / (jnp.sqrt(moment_two) + ADAM_EPS) + DECAY_RATE * params)
    return (params, moment_one, moment_two)

def reference(outer_params, outer_momentum, inner_mean, inner_square, latents, noise_draw, timesteps, fragment, modulation):
    mod_rows = lax.dynamic_index_in_dim(modulation, fragment[0].astype(jnp.int32), 0, keepdims=False)
    mod_shift = mod_rows[0]
    mod_scale = mod_rows[1]
    total_rows = TOK_DEV * N_FSDP
    lat_split = latents.reshape(STEPS, N_REPLICA, N_FSDP, TOK_DEV, CH).transpose(1, 0, 2, 3, 4)
    noise_split = noise_draw.reshape(STEPS, N_REPLICA, N_FSDP, TOK_DEV, CH).transpose(1, 0, 2, 3, 4)
    level_split = timesteps.reshape(STEPS, N_REPLICA, N_FSDP, TOK_DEV).transpose(1, 0, 2, 3)

    def replica_run(inputs):
        moment_one, moment_two, lat_rep, noise_rep, level_rep = inputs
        params = outer_params
        for inner_step in range(STEPS):
            weights = params.astype(jnp.bfloat16)

            def add_block(total, block):
                partial_grad = local_grads(weights, block[0], block[1], block[2], mod_shift, mod_scale, total_rows)
                rounded = lax.optimization_barrier(partial_grad.astype(jnp.bfloat16))
                return (total + rounded.astype(jnp.float32), None)
            gradient, _ = lax.scan(add_block, jnp.zeros((FRAG_ROWS, D), jnp.float32), (lat_rep[inner_step], noise_rep[inner_step], level_rep[inner_step]))
            params, moment_one, moment_two = adam_update(params, moment_one, moment_two, gradient)
        return (params, moment_one, moment_two)
    final_params, new_mean, new_square = lax.map(replica_run, (inner_mean, inner_square, lat_split, noise_split, level_split))
    pseudo = lax.optimization_barrier(jnp.sum(outer_params[None] - final_params, axis=0)) / N_REPLICA
    new_momentum = NESTEROV * outer_momentum + pseudo
    new_params = outer_params - OUTER_RATE * (pseudo + NESTEROV * new_momentum)
    return (new_params, new_momentum, new_mean, new_square)
```

```python
import math

import jax
import jax.numpy as jnp
from jax import lax
from jax.sharding import PartitionSpec as P

STEPS = 2
LEVELS = 1000


BETA_ONE = 0.9
BETA_TWO = 0.95
INNER_RATE = 0.2
DECAY_RATE = 0.1
ADAM_EPS = 1e-08
NORM_EPS = 1e-06
OUTER_RATE = 0.7
NESTEROV = 0.9

CORES = 2


def core_swap(values, width):
    return lax.ppermute(values, "fsdp", [(i, i ^ 1) for i in range(width)])


def chip_exchange(blocks, width):
    groups = [list(range(core, width, CORES)) for core in range(CORES)]
    return lax.all_to_all(blocks, "fsdp", 0, 0, axis_index_groups=groups)


def split_halves(values, core):
    half = values.shape[-1] // CORES
    mine = lax.dynamic_slice_in_dim(values, core * half, half, values.ndim - 1)
    other = lax.dynamic_slice_in_dim(values, (1 - core) * half, half, values.ndim - 1)
    return mine, other


def to_pair(values, core, width):
    mine, other = split_halves(values, core)
    received = core_swap(other, width)
    first = jnp.where(core == 0, mine, received)
    second = jnp.where(core == 0, received, mine)
    return jnp.concatenate([first, second], axis=0)


def from_pair(values, core, width):
    rows = values.shape[0] // CORES
    mine = lax.dynamic_slice_in_dim(values, core * rows, rows, 0)
    other = lax.dynamic_slice_in_dim(values, (1 - core) * rows, rows, 0)
    received = core_swap(other, width)
    first = jnp.where(core == 0, mine, received)
    second = jnp.where(core == 0, received, mine)
    return jnp.concatenate([first, second], axis=1)


def embed_levels(levels, time_width):
    half_width = time_width // 2
    noise_level = (levels.astype(jnp.float32) + 0.5) / LEVELS
    frequencies = jnp.exp(
        -math.log(10000.0) * jnp.arange(half_width, dtype=jnp.float32) / half_width
    )
    angles = (1000.0 * noise_level)[:, None] * frequencies[None, :]
    return (jnp.concatenate([jnp.cos(angles), jnp.sin(angles)], axis=-1), noise_level)


def local_grads(weights, latent_rows, noise_rows, levels, mod_shift, mod_scale, total_rows):
    channels = latent_rows.shape[1]
    model_width = weights.shape[1]
    time_width = weights.shape[0] - 2 * channels
    in_weight = weights[:channels]
    time_weight = weights[channels : channels + time_width]
    out_weight = weights[channels + time_width :]
    level_embed, noise_level = embed_levels(levels, time_width)
    latent_f = latent_rows.astype(jnp.float32)
    noise_f = noise_rows.astype(jnp.float32)
    noised = ((1.0 - noise_level)[:, None] * latent_f + noise_level[:, None] * noise_f).astype(
        jnp.bfloat16
    )
    target = noise_f - latent_f
    embed_b = level_embed.astype(jnp.bfloat16)
    time_pre = jnp.dot(embed_b, time_weight, preferred_element_type=jnp.float32) / math.sqrt(
        time_width
    )
    hidden = jnp.dot(noised, in_weight, preferred_element_type=jnp.float32) / math.sqrt(
        channels
    ) + jax.nn.silu(time_pre)
    inverse = lax.rsqrt(jnp.mean(hidden * hidden, axis=-1, keepdims=True) + NORM_EPS)
    normed = hidden * inverse
    factor = 1.0 + mod_scale
    modded = (normed * factor + mod_shift).astype(jnp.bfloat16)
    output = lax.dot_general(
        modded, out_weight, (((1,), (1,)), ((), ())), preferred_element_type=jnp.float32
    ) / math.sqrt(model_width)
    out_grad = (2.0 / (total_rows * channels) * (output - target)).astype(jnp.bfloat16)
    grad_out = lax.dot_general(
        out_grad, modded, (((0,), (0,)), ((), ())), preferred_element_type=jnp.float32
    ) / math.sqrt(model_width)
    mod_grad = jnp.dot(out_grad, out_weight, preferred_element_type=jnp.float32) / math.sqrt(
        model_width
    )
    norm_grad = mod_grad * factor
    hid_grad = inverse * (norm_grad - normed * jnp.mean(norm_grad * normed, axis=-1, keepdims=True))
    sigmoid_pre = jax.nn.sigmoid(time_pre)
    pre_grad = hid_grad * (sigmoid_pre * (1.0 + time_pre * (1.0 - sigmoid_pre)))
    grad_in = lax.dot_general(
        noised,
        hid_grad.astype(jnp.bfloat16),
        (((0,), (0,)), ((), ())),
        preferred_element_type=jnp.float32,
    ) / math.sqrt(channels)
    grad_time = lax.dot_general(
        embed_b,
        pre_grad.astype(jnp.bfloat16),
        (((0,), (0,)), ((), ())),
        preferred_element_type=jnp.float32,
    ) / math.sqrt(time_width)
    return jnp.concatenate([grad_in, grad_time, grad_out], axis=0)


def adam_update(params, moment_one, moment_two, gradient):
    moment_one = BETA_ONE * moment_one + (1.0 - BETA_ONE) * gradient
    moment_two = BETA_TWO * moment_two + (1.0 - BETA_TWO) * gradient * gradient
    params = params - INNER_RATE * (
        moment_one / (jnp.sqrt(moment_two) + ADAM_EPS) + DECAY_RATE * params
    )
    return (params, moment_one, moment_two)


def gather_weights(params, width):
    chips = width // CORES
    block = params.astype(jnp.bfloat16)
    gathered = chip_exchange(jnp.broadcast_to(block[None], (chips,) + block.shape), width)
    gathered = gathered.reshape(chips * block.shape[0], block.shape[1])
    return jnp.concatenate([gathered, core_swap(gathered, width)], axis=1)


def scatter_gradient(gradient, width):
    chips = width // CORES
    half = gradient.shape[1] // CORES
    received = core_swap(gradient[:, half:].astype(jnp.bfloat16), width)
    pair_sum = (gradient[:, :half] + received.astype(jnp.float32)).astype(jnp.bfloat16)
    blocks = chip_exchange(pair_sum.reshape(chips, gradient.shape[0] // chips, half), width)
    return jnp.sum(blocks.astype(jnp.float32), axis=0)


def replica_sum(values):
    replicas = lax.axis_size("replica")
    rows, columns = values.shape
    parts = 4
    strips = replicas // parts
    block = values.astype(jnp.bfloat16).reshape(parts, rows // parts, strips, columns // strips)
    block = block.transpose(0, 2, 1, 3).reshape(replicas, rows // parts, columns // strips)
    block = lax.all_to_all(block, "replica", 0, 0)
    total = jnp.sum(block.astype(jnp.float32), axis=0).astype(jnp.bfloat16)
    total = lax.all_to_all(jnp.broadcast_to(total[None], block.shape), "replica", 0, 0)
    total = total.reshape(parts, strips, rows // parts, columns // strips).transpose(0, 2, 1, 3)
    return total.reshape(rows, columns).astype(jnp.float32)


def on_device(
    outer_params,
    outer_momentum,
    inner_mean,
    inner_square,
    latents,
    noise_draw,
    timesteps,
    fragment,
    modulation,
):
    width = lax.axis_size("fsdp")
    core = lax.axis_index("fsdp") % CORES
    mod_rows = lax.dynamic_index_in_dim(modulation, fragment[0], 0, keepdims=False)
    mod_rows = jnp.concatenate(split_halves(mod_rows, core), axis=1)
    mod_shift = mod_rows[0]
    mod_scale = mod_rows[1]
    total_rows = latents.shape[1] * width
    start = to_pair(outer_params, core, width)
    params = start
    moment_one = to_pair(inner_mean[0], core, width)
    moment_two = to_pair(inner_square[0], core, width)
    for inner_step in range(STEPS):
        weights = gather_weights(params, width)
        grad_local = local_grads(
            weights,
            latents[inner_step],
            noise_draw[inner_step],
            timesteps[inner_step],
            mod_shift,
            mod_scale,
            total_rows,
        )
        gradient = scatter_gradient(grad_local, width)
        params, moment_one, moment_two = adam_update(params, moment_one, moment_two, gradient)
    new_mean = from_pair(moment_one, core, width)
    new_square = from_pair(moment_two, core, width)
    average = replica_sum(start - params) / lax.axis_size("replica")
    average = from_pair(average, core, width)
    new_momentum = NESTEROV * outer_momentum + average
    new_params = outer_params - OUTER_RATE * (average + NESTEROV * new_momentum)
    return (new_params, new_momentum, new_mean[None], new_square[None])


def solution(mesh):
    return jax.shard_map(
        on_device,
        mesh=mesh,
        in_specs=(
            P("fsdp", None),
            P("fsdp", None),
            P("replica", "fsdp", None),
            P("replica", "fsdp", None),
            P(None, ("replica", "fsdp"), None),
            P(None, ("replica", "fsdp"), None),
            P(None, ("replica", "fsdp")),
            P(),
            P(),
        ),
        out_specs=(
            P("fsdp", None),
            P("fsdp", None),
            P("replica", "fsdp", None),
            P("replica", "fsdp", None),
        ),
        check_vma=False,
    )
```

```python
import math

import jax
import jax.numpy as jnp
from jax import lax
from jax.experimental import pallas as pl
from jax.experimental.pallas import tpu as pltpu
from jax.sharding import PartitionSpec as P

STEPS = 2
LEVELS = 1000


BETA_ONE = 0.9
BETA_TWO = 0.95
INNER_RATE = 0.2
DECAY_RATE = 0.1
ADAM_EPS = 1e-08
NORM_EPS = 1e-06
OUTER_RATE = 0.7
NESTEROV = 0.9

CORES = 2
LANES = 128
ROW_CHUNK = 16
FWD_COLUMNS = 256
STRIP_ROWS = 16
STRIP_PARTS = 4
KERNEL_VMEM = 24 * 2**20

BF16 = jnp.bfloat16
F32 = jnp.float32
VMEM = pl.BlockSpec(memory_space=pltpu.VMEM)
SMEM = pl.BlockSpec(memory_space=pltpu.SMEM)
TRANSPOSED = (((1,), (1,)), ((), ()))


def local_call(kernel, name, args, outs, scratch=(), core=None, flops=0, hbm_outs=False):
    place = pltpu.VMEM if not hbm_outs else jax.ShapeDtypeStruct
    specs = [VMEM] * len(args)
    values = [pltpu.with_memory_space_constraint(a, pltpu.VMEM) for a in args]
    if core is not None:
        specs = [SMEM] + specs
        values = [core] + values
    moved = sum(math.prod(o[0]) * 4 for o in outs) + sum(a.size * a.dtype.itemsize for a in args)
    return pl.pallas_call(
        kernel,
        in_specs=specs,
        out_specs=[VMEM] * len(outs),
        out_shape=[place(shape, dtype) for shape, dtype in outs],
        scratch_shapes=list(scratch),
        compiler_params=pltpu.CompilerParams(vmem_limit_bytes=KERNEL_VMEM),
        cost_estimate=pl.CostEstimate(flops=flops, bytes_accessed=moved, transcendentals=0),
        name=name,
    )(*values)


def core_swap(values, width):
    return lax.ppermute(values, "fsdp", [(i, i ^ 1) for i in range(width)])


def chip_exchange(blocks, width):
    groups = [list(range(core, width, CORES)) for core in range(CORES)]
    return lax.all_to_all(blocks, "fsdp", 0, 0, axis_index_groups=groups)


def pair_kernel(core, own, got, pair, *copies):
    rows = own.shape[0]
    half = own.shape[1] // CORES

    @pl.when(core[0] == 0)
    def _():
        pair[0:rows] = own[:, 0:half]
        pair[rows:] = got[:, 0:half]

    @pl.when(core[0] != 0)
    def _():
        pair[0:rows] = got[:, half:]
        pair[rows:] = own[:, half:]

    for copy in copies:
        block = pair[...].astype(BF16)
        for chip in range(copy.shape[0]):
            copy[chip] = block


def to_pair(values, core, width, copies=()):
    rows, columns = values.shape
    shape = (rows * CORES, columns // CORES)
    outs = [(shape, F32)] + [((n,) + shape, BF16) for n in copies]
    return local_call(pair_kernel, "pair", (values, core_swap(values, width)), outs, core=core)


def unpair_kernel(core, own, got, out):
    rows = out.shape[0]
    half = out.shape[1] // CORES

    @pl.when(core[0] == 0)
    def _():
        out[:, 0:half] = own[0:rows]
        out[:, half:] = got[0:rows]

    @pl.when(core[0] != 0)
    def _():
        out[:, 0:half] = got[rows:]
        out[:, half:] = own[rows:]


def from_pair(values, core, width):
    rows, columns = values.shape
    outs = [((rows // CORES, columns * CORES), F32)]
    args = (values, core_swap(values, width))
    return local_call(unpair_kernel, "unpair", args, outs, core=core, hbm_outs=True)[0]


def forward_kernel(tokens, embed, weights, factor, shift, hid, mod, slope, out, square, bias, pre_buf, in_buf):
    channels = tokens.shape[1]
    time_end = channels + embed.shape[1]
    square[...] = jnp.zeros_like(square)
    for index in range(weights.shape[1] // FWD_COLUMNS):
        slot = index % 2
        cols = pl.ds(index * FWD_COLUMNS, FWD_COLUMNS)
        pre_buf[slot] = jnp.dot(
            embed[...], weights[channels:time_end, cols], preferred_element_type=F32
        )
        in_buf[slot] = jnp.dot(tokens[...], weights[0:channels, cols], preferred_element_type=F32)
        scale = jnp.broadcast_to(factor[0:1, cols], (ROW_CHUNK, FWD_COLUMNS))
        for start in range(0, tokens.shape[0], ROW_CHUNK):
            rows = pl.ds(start, ROW_CHUNK)
            pre = pre_buf[slot, rows, :]
            sigma = 0.5 * jnp.tanh(0.5 * pre) + 0.5
            silu = pre * sigma
            hidden = in_buf[slot, rows, :] + silu
            mod[rows, cols] = (hidden * scale).astype(BF16)
            hid[rows, cols] = hidden.astype(BF16)
            slope[rows, cols] = (sigma + (silu - silu * sigma)).astype(BF16)
            power = hidden * hidden
            partial = power[:, 0:LANES]
            for lane in range(LANES, FWD_COLUMNS, LANES):
                partial = partial + power[:, lane : lane + LANES]
            square[rows, :] += partial
    out_weight = weights[time_end:, :]
    out[...] = lax.dot_general(mod[...], out_weight, TRANSPOSED, preferred_element_type=F32)
    bias[...] = lax.dot_general(shift[...], out_weight, TRANSPOSED, preferred_element_type=F32)


def forward(tokens, embed, weights, factor, shift):
    rows, columns = tokens.shape[0], weights.shape[1]
    channels = tokens.shape[1]
    outs = [((rows, columns), BF16)] * 3 + [
        ((rows, channels), F32),
        ((rows, LANES), F32),
        ((shift.shape[0], channels), F32),
    ]
    scratch = [pltpu.VMEM((2, rows, FWD_COLUMNS), F32)] * 2
    flops = 2 * rows * columns * weights.shape[0]
    args = (tokens, embed, weights, factor, shift)
    return local_call(forward_kernel, "forward", args, outs, scratch, flops=flops)


def make_head_kernel(model_width, total_rows):
    def head_kernel(out_a, out_b, square_a, square_b, bias_a, bias_b, target, grad, grad_t, pull, grad_sum):
        root = 1.0 / math.sqrt(model_width)
        raw = out_a[...] + out_b[...]
        power = jnp.sum(square_a[...] + square_b[...], axis=1, keepdims=True)
        inverse = lax.rsqrt(power * (1.0 / model_width) + NORM_EPS)
        bias = jnp.sum(bias_a[...] + bias_b[...], axis=0, keepdims=True)
        output = (inverse * raw + bias) * root
        out_grad = (2.0 / (total_rows * raw.shape[1])) * (output - target[...])
        scaled = (out_grad * inverse).astype(BF16)
        wide = scaled.astype(F32)
        grad[...] = scaled
        grad_t[...] = wide.T.astype(BF16)
        pulled = inverse * inverse * (root / model_width) * jnp.sum(wide * raw, axis=1, keepdims=True)
        pull[...] = jnp.broadcast_to(pulled, pull.shape)
        summed = jnp.sum(out_grad.T, axis=1, keepdims=True)
        grad_sum[...] = jnp.broadcast_to(summed, grad_sum.shape)

    return head_kernel


def make_backward_kernel(model_width):
    def backward_kernel(
        hid, mod, slope, weights, factor, shift, tokens_t, embed_t, grad, grad_t, pull, grad_sum,
        out, mod_buf, hid_buf, pre_buf,
    ):
        root = 1.0 / math.sqrt(model_width)
        channels = tokens_t.shape[0]
        time_end = channels + embed_t.shape[0]
        columns = out.shape[1]
        mod_buf[...] = jnp.dot(grad[...], weights[time_end:, :], preferred_element_type=F32)
        scale = jnp.broadcast_to(factor[0:1, :] * root, (ROW_CHUNK, columns))
        for start in range(0, grad.shape[0], ROW_CHUNK):
            rows = pl.ds(start, ROW_CHUNK)
            pulled = jnp.concatenate([pull[rows, :]] * (columns // LANES), axis=1)
            hid_grad = mod_buf[rows, :] * scale - hid[rows, :].astype(F32) * pulled
            hid_buf[rows, :] = hid_grad.astype(BF16)
            pre_buf[rows, :] = (hid_grad * slope[rows, :].astype(F32)).astype(BF16)
        out[0:channels, :] = jnp.dot(
            tokens_t[...], hid_buf[...], preferred_element_type=F32
        ).astype(BF16)
        out[channels:time_end, :] = jnp.dot(
            embed_t[...], pre_buf[...], preferred_element_type=F32
        ).astype(BF16)
        grad_out = jnp.dot(grad_t[...], mod[...], preferred_element_type=F32)
        summed = jnp.concatenate([grad_sum[...]] * (columns // LANES), axis=1)
        out[time_end:, :] = ((grad_out + summed * shift[0:1, :]) * root).astype(BF16)

    return backward_kernel


def backward(state, weights, factor, shift, tokens_t, embed_t, head, model_width):
    rows, columns = state[0].shape
    scratch = [
        pltpu.VMEM((rows, columns), F32),
        pltpu.VMEM((rows, columns), BF16),
        pltpu.VMEM((rows, columns), BF16),
    ]
    flops = 2 * rows * columns * (weights.shape[0] + tokens_t.shape[0])
    args = (*state, weights, factor, shift, tokens_t, embed_t, *head)
    outs = [(weights.shape, BF16)]
    return local_call(make_backward_kernel(model_width), "backward", args, outs, scratch, flops=flops)[0]


def prepare_tokens(latent_rows, noise_rows, levels, channels, time_width):
    half_width = time_width // 2
    noise_level = (levels.astype(F32) + 0.5) / LEVELS
    frequencies = jnp.exp(-math.log(10000.0) * jnp.arange(half_width, dtype=F32) / half_width)
    angles = (1000.0 * noise_level)[:, None] * frequencies[None, :]
    embed = jnp.concatenate([jnp.cos(angles), jnp.sin(angles)], axis=-1).astype(BF16)
    latent_f = latent_rows.astype(F32)
    noise_f = noise_rows.astype(F32)
    noised = ((1.0 - noise_level)[:, None] * latent_f + noise_level[:, None] * noise_f).astype(BF16)
    noised = noised * BF16(1.0 / math.sqrt(channels))
    embed = embed * BF16(1.0 / math.sqrt(time_width))
    return noised, embed, noised.T, embed.T, noise_f - latent_f


def step_kernel(blocks, params, mean, square, new_mean, new_square, new_params, copies):
    first, second, new = adam(blocks, params, mean, square)
    new_mean[...] = first
    new_square[...] = second
    new_params[...] = new
    block = new.astype(BF16)
    for chip in range(copies.shape[0]):
        copies[chip] = block


def last_kernel(blocks, params, mean, square, start, new_mean, new_square, strips):
    first, second, new = adam(blocks, params, mean, square)
    new_mean[...] = first
    new_square[...] = second
    drift = (start[...] - new).astype(BF16)
    rows, columns = strips.shape[1:]
    used = 0
    for top in range(0, drift.shape[0], rows):
        for left in range(0, drift.shape[1], columns):
            strips[used] = drift[top : top + rows, left : left + columns]
            used += 1
    for index in range(used, strips.shape[0]):
        strips[index] = jnp.zeros((rows, columns), BF16)


def adam(blocks, params, mean, square):
    gradient = blocks[0].astype(F32)
    for chip in range(1, blocks.shape[0]):
        gradient = gradient + blocks[chip].astype(F32)
    old = params[...]
    first = BETA_ONE * mean[...] + (1.0 - BETA_ONE) * gradient
    second = BETA_TWO * square[...] + (1.0 - BETA_TWO) * gradient * gradient
    new = old - INNER_RATE * (first / (jnp.sqrt(second) + ADAM_EPS) + DECAY_RATE * old)
    return first, second, new


def strip_sum_kernel(strips, copies):
    total = strips[0].astype(F32)
    for index in range(1, strips.shape[0]):
        total = total + strips[index].astype(F32)
    block = total.astype(BF16)
    for index in range(copies.shape[0]):
        copies[index] = block


def make_outer_kernel(replicas):
    def outer_kernel(core, own, got, params, momentum, new_params, new_momentum, own_buf, got_buf):
        strip_rows, strip_columns = own.shape[1:]
        rows = params.shape[0]
        half = params.shape[1] // CORES
        index = 0
        for top in range(0, rows * CORES, strip_rows):
            for left in range(0, half, strip_columns):
                place = (slice(top, top + strip_rows), slice(left, left + strip_columns))
                own_buf[place] = own[index].astype(F32)
                got_buf[place] = got[index].astype(F32)
                index += 1

        def finish(cols, values):
            average = values * (1.0 / replicas)
            moved = NESTEROV * momentum[:, cols] + average
            new_momentum[:, cols] = moved
            new_params[:, cols] = params[:, cols] - OUTER_RATE * (average + NESTEROV * moved)

        @pl.when(core[0] == 0)
        def _():
            finish(slice(0, half), own_buf[0:rows])
            finish(slice(half, 2 * half), got_buf[0:rows])

        @pl.when(core[0] != 0)
        def _():
            finish(slice(0, half), got_buf[rows:])
            finish(slice(half, 2 * half), own_buf[rows:])

    return outer_kernel


def on_device(
    outer_params,
    outer_momentum,
    inner_mean,
    inner_square,
    latents,
    noise_draw,
    timesteps,
    fragment,
    modulation,
):
    width = lax.axis_size("fsdp")
    replicas = lax.axis_size("replica")
    chips = width // CORES
    core = (lax.axis_index("fsdp") % CORES).astype(jnp.int32)
    core_arg = core.reshape(1)
    rows, model_width = outer_params.shape
    half = model_width // CORES
    channels = latents.shape[2]
    time_width = rows * width - 2 * channels
    total_rows = latents.shape[1] * width

    start, copies = to_pair(outer_params, core_arg, width, (chips,))
    gathered = chip_exchange(copies, width)

    mod_rows = lax.dynamic_index_in_dim(modulation, fragment[0], 0, keepdims=False)
    mods = []
    for side in (core, 1 - core):
        rows_here = lax.dynamic_slice_in_dim(mod_rows, side * half, half, 1)
        shift = rows_here[0:1]
        high = shift.astype(BF16)
        low = (shift - high.astype(F32)).astype(BF16)
        terms = jnp.concatenate([high, low, jnp.zeros((14, half), BF16)], axis=0)
        mods.append((1.0 + rows_here[1:2], shift, terms))
    prepared = [
        prepare_tokens(latents[s], noise_draw[s], timesteps[s], channels, time_width)
        for s in range(STEPS)
    ]
    params = start
    mean = to_pair(inner_mean[0], core_arg, width)[0]
    square = to_pair(inner_square[0], core_arg, width)[0]
    pair_shape = start.shape

    for step in range(STEPS):
        tokens, embed, tokens_t, embed_t, target = prepared[step]
        weights = gathered.reshape(chips * pair_shape[0], half)
        other = core_swap(weights, width)
        state = forward(tokens, embed, weights, mods[0][0], mods[0][2])
        state_other = forward(tokens, embed, other, mods[1][0], mods[1][2])
        shapes = [
            ((target.shape[0], channels), BF16),
            ((channels, target.shape[0]), BF16),
            ((target.shape[0], LANES), F32),
            ((channels, LANES), F32),
        ]
        head = local_call(
            make_head_kernel(model_width, total_rows),
            "head",
            (state[3], state_other[3], state[4], state_other[4], state[5], state_other[5], target),
            shapes,
        )
        grad_other = backward(
            state_other[:3], other, mods[1][0], mods[1][1], tokens_t, embed_t, head, model_width
        )
        received = core_swap(grad_other, width)
        head, grad_other = lax.optimization_barrier((head, grad_other))
        grad_mine = backward(
            state[:3], weights, mods[0][0], mods[0][1], tokens_t, embed_t, head, model_width
        )
        pair_sum = (grad_mine.astype(F32) + received.astype(F32)).astype(BF16)
        blocks = chip_exchange(pair_sum.reshape((chips,) + pair_shape), width)
        moments = [(pair_shape, F32)] * 2
        if step + 1 < STEPS:
            outs = moments + [(pair_shape, F32), ((chips,) + pair_shape, BF16)]
            mean, square, params, copies = local_call(
                step_kernel, "update", (blocks, params, mean, square), outs
            )
            gathered = chip_exchange(copies, width)
        else:
            strip = (STRIP_ROWS, half // STRIP_PARTS)
            outs = moments + [((replicas,) + strip, BF16)]
            mean, square, strips = local_call(
                last_kernel, "update_last", (blocks, params, mean, square, start), outs
            )
    strips = lax.all_to_all(strips, "replica", 0, 0)
    strips = local_call(strip_sum_kernel, "strip_sum", (strips,), [(strips.shape, BF16)])[0]
    strips = lax.all_to_all(strips, "replica", 0, 0)
    new_mean = from_pair(mean, core_arg, width)
    new_square = from_pair(square, core_arg, width)
    new_params, new_momentum = local_call(
        make_outer_kernel(replicas),
        "outer",
        (strips, core_swap(strips, width), outer_params, outer_momentum),
        [(outer_params.shape, F32)] * 2,
        [pltpu.VMEM(pair_shape, F32)] * 2,
        core=core_arg,
        hbm_outs=True,
    )
    return (new_params, new_momentum, new_mean[None], new_square[None])


def solution(mesh):
    return jax.shard_map(
        on_device,
        mesh=mesh,
        in_specs=(
            P("fsdp", None),
            P("fsdp", None),
            P("replica", "fsdp", None),
            P("replica", "fsdp", None),
            P(None, ("replica", "fsdp"), None),
            P(None, ("replica", "fsdp"), None),
            P(None, ("replica", "fsdp")),
            P(),
            P(),
        ),
        out_specs=(
            P("fsdp", None),
            P("fsdp", None),
            P("replica", "fsdp", None),
            P("replica", "fsdp", None),
        ),
        check_vma=False,
    )
```

```python
import math

import jax
import jax.numpy as jnp
from jax import lax
from jax.experimental import pallas as pl
from jax.experimental.pallas import tpu as pltpu
from jax.sharding import PartitionSpec as P

STEPS = 2
LEVELS = 1000


BETA_ONE = 0.9
BETA_TWO = 0.95
INNER_RATE = 0.2
DECAY_RATE = 0.1
ADAM_EPS = 1e-08
NORM_EPS = 1e-06
OUTER_RATE = 0.7
NESTEROV = 0.9

CORES = 2
LANES = 128
ROW_CHUNK = 16
FWD_COLUMNS = 256
STRIP_ROWS = 16
STRIP_PARTS = 4
KERNEL_VMEM = 24 * 2**20

BF16 = jnp.bfloat16
F32 = jnp.float32
VMEM = pl.BlockSpec(memory_space=pltpu.VMEM)
SMEM = pl.BlockSpec(memory_space=pltpu.SMEM)
TRANSPOSED = (((1,), (1,)), ((), ()))


def local_call(kernel, name, args, outs, scratch=(), scalars=(), flops=0, hbm_outs=False):
    place = pltpu.VMEM if not hbm_outs else jax.ShapeDtypeStruct
    specs = [SMEM] * len(scalars) + [VMEM] * len(args)
    values = [*scalars, *(pltpu.with_memory_space_constraint(a, pltpu.VMEM) for a in args)]
    moved = sum(math.prod(o[0]) * 4 for o in outs) + sum(a.size * a.dtype.itemsize for a in args)
    return pl.pallas_call(
        kernel,
        in_specs=specs,
        out_specs=[VMEM] * len(outs),
        out_shape=[place(shape, dtype) for shape, dtype in outs],
        scratch_shapes=list(scratch),
        compiler_params=pltpu.CompilerParams(vmem_limit_bytes=KERNEL_VMEM),
        cost_estimate=pl.CostEstimate(flops=flops, bytes_accessed=moved, transcendentals=0),
        name=name,
    )(*values)


def core_swap(values, width):
    return lax.ppermute(values, "fsdp", [(i, i ^ 1) for i in range(width)])


def chip_exchange(blocks, width):
    groups = [list(range(core, width, CORES)) for core in range(CORES)]
    return lax.all_to_all(blocks, "fsdp", 0, 0, axis_index_groups=groups)


def hold_kernel(values, held):
    held[...] = values[...]


def hold(values):
    return local_call(hold_kernel, "hold", (values,), [(values.shape, values.dtype)])[0]


def pair_halves(core, own, got, pair):
    rows = own.shape[0]
    half = own.shape[1] // CORES

    @pl.when(core[0] == 0)
    def _():
        pair[0:rows] = own[:, 0:half]
        pair[rows:] = got[:, 0:half]

    @pl.when(core[0] != 0)
    def _():
        pair[0:rows] = got[:, half:]
        pair[rows:] = own[:, half:]


def start_kernel(core, own, got, pair, copies):
    pair_halves(core, own, got, pair)
    block = pair[...].astype(BF16)
    for chip in range(copies.shape[0]):
        copies[chip] = block


def moments_kernel(core, mean, mean_got, square, square_got, mean_pair, square_pair):
    pair_halves(core, mean, mean_got, mean_pair)
    pair_halves(core, square, square_got, square_pair)


def unpair_halves(core, own, got, out):
    rows = out.shape[0]
    half = out.shape[1] // CORES

    @pl.when(core[0] == 0)
    def _():
        out[:, 0:half] = own[0:rows]
        out[:, half:] = got[0:rows]

    @pl.when(core[0] != 0)
    def _():
        out[:, 0:half] = got[rows:]
        out[:, half:] = own[rows:]


def unpair_kernel(core, mean, mean_got, square, square_got, new_mean, new_square):
    unpair_halves(core, mean, mean_got, new_mean)
    unpair_halves(core, square, square_got, new_square)


def forward_kernel(tokens, embed, weights, factor, shift, hid, mod, slope, out, square, bias, pre_buf, in_buf):
    channels = tokens.shape[1]
    time_end = channels + embed.shape[1]
    square[...] = jnp.zeros_like(square)
    for index in range(weights.shape[1] // FWD_COLUMNS):
        slot = index % 2
        cols = pl.ds(index * FWD_COLUMNS, FWD_COLUMNS)
        pre_buf[slot] = jnp.dot(
            embed[...], weights[channels:time_end, cols], preferred_element_type=F32
        )
        in_buf[slot] = jnp.dot(tokens[...], weights[0:channels, cols], preferred_element_type=F32)
        scale = jnp.broadcast_to(factor[0:1, cols], (ROW_CHUNK, FWD_COLUMNS))
        for start in range(0, tokens.shape[0], ROW_CHUNK):
            rows = pl.ds(start, ROW_CHUNK)
            pre = pre_buf[slot, rows, :]
            sigma = 0.5 * jnp.tanh(0.5 * pre) + 0.5
            silu = pre * sigma
            hidden = in_buf[slot, rows, :] + silu
            mod[rows, cols] = (hidden * scale).astype(BF16)
            hid[rows, cols] = hidden.astype(BF16)
            slope[rows, cols] = (sigma + (silu - silu * sigma)).astype(BF16)
            power = hidden * hidden
            partial = power[:, 0:LANES]
            for lane in range(LANES, FWD_COLUMNS, LANES):
                partial = partial + power[:, lane : lane + LANES]
            square[rows, :] += partial
    out_weight = weights[time_end:, :]
    out[...] = lax.dot_general(mod[...], out_weight, TRANSPOSED, preferred_element_type=F32)
    bias[...] = lax.dot_general(shift[...], out_weight, TRANSPOSED, preferred_element_type=F32)


def forward(tokens, embed, weights, factor, shift):
    rows, columns = tokens.shape[0], weights.shape[1]
    channels = tokens.shape[1]
    outs = [((rows, columns), BF16)] * 3 + [
        ((rows, channels), F32),
        ((rows, LANES), F32),
        ((shift.shape[0], channels), F32),
    ]
    scratch = [pltpu.VMEM((2, rows, FWD_COLUMNS), F32)] * 2
    flops = 2 * rows * columns * weights.shape[0]
    args = (tokens, embed, weights, factor, shift)
    return local_call(forward_kernel, "forward", args, outs, scratch, flops=flops)


def make_head_kernel(model_width, total_rows):
    def head_kernel(out_a, out_b, square_a, square_b, bias_a, bias_b, target, grad, grad_t, pull, grad_sum):
        root = 1.0 / math.sqrt(model_width)
        raw = out_a[...] + out_b[...]
        power = jnp.sum(square_a[...] + square_b[...], axis=1, keepdims=True)
        inverse = lax.rsqrt(power * (1.0 / model_width) + NORM_EPS)
        bias = jnp.sum(bias_a[...] + bias_b[...], axis=0, keepdims=True)
        output = (inverse * raw + bias) * root
        out_grad = (2.0 / (total_rows * raw.shape[1])) * (output - target[...])
        scaled = (out_grad * inverse).astype(BF16)
        wide = scaled.astype(F32)
        grad[...] = scaled
        grad_t[...] = wide.T.astype(BF16)
        pulled = inverse * inverse * (root / model_width) * jnp.sum(wide * raw, axis=1, keepdims=True)
        pull[...] = jnp.broadcast_to(pulled, pull.shape)
        summed = jnp.sum(out_grad.T, axis=1, keepdims=True)
        grad_sum[...] = jnp.broadcast_to(summed, grad_sum.shape)

    return head_kernel


def make_backward_kernel(model_width):
    def backward_kernel(
        hid, mod, slope, weights, factor, shift, tokens_t, embed_t, grad, grad_t, pull, grad_sum,
        out, mod_buf, hid_buf, pre_buf,
    ):
        root = 1.0 / math.sqrt(model_width)
        channels = tokens_t.shape[0]
        time_end = channels + embed_t.shape[0]
        columns = out.shape[1]
        mod_buf[...] = jnp.dot(grad[...], weights[time_end:, :], preferred_element_type=F32)
        scale = jnp.broadcast_to(factor[0:1, :] * root, (ROW_CHUNK, columns))
        for start in range(0, grad.shape[0], ROW_CHUNK):
            rows = pl.ds(start, ROW_CHUNK)
            pulled = jnp.concatenate([pull[rows, :]] * (columns // LANES), axis=1)
            hid_grad = mod_buf[rows, :] * scale - hid[rows, :].astype(F32) * pulled
            hid_buf[rows, :] = hid_grad.astype(BF16)
            pre_buf[rows, :] = (hid_grad * slope[rows, :].astype(F32)).astype(BF16)
        out[0:channels, :] = jnp.dot(
            tokens_t[...], hid_buf[...], preferred_element_type=F32
        ).astype(BF16)
        out[channels:time_end, :] = jnp.dot(
            embed_t[...], pre_buf[...], preferred_element_type=F32
        ).astype(BF16)
        grad_out = jnp.dot(grad_t[...], mod[...], preferred_element_type=F32)
        summed = jnp.concatenate([grad_sum[...]] * (columns // LANES), axis=1)
        out[time_end:, :] = ((grad_out + summed * shift[0:1, :]) * root).astype(BF16)

    return backward_kernel


def backward(state, weights, factor, shift, tokens_t, embed_t, head, model_width):
    rows, columns = state[0].shape
    scratch = [
        pltpu.VMEM((rows, columns), F32),
        pltpu.VMEM((rows, columns), BF16),
        pltpu.VMEM((rows, columns), BF16),
    ]
    flops = 2 * rows * columns * (weights.shape[0] + tokens_t.shape[0])
    args = (*state, weights, factor, shift, tokens_t, embed_t, *head)
    outs = [(weights.shape, BF16)]
    return local_call(make_backward_kernel(model_width), "backward", args, outs, scratch, flops=flops)[0]


def prepare_kernel(core, fragment, latents, noise, levels, modulation, *outs):
    steps, channels, tokens = latents.shape
    half_width = outs[1].shape[1] // 2
    per_step = 5
    for step in range(steps):
        token_rows, embed_rows, token_cols, embed_cols, target = outs[per_step * step : per_step * (step + 1)]
        level = (levels[step : step + 1, :].astype(F32) + 0.5) / LEVELS
        latent = latents[step].astype(F32)
        draw = noise[step].astype(F32)
        noised = ((1.0 - level) * latent + level * draw).astype(BF16).astype(F32)
        noised = noised * (1.0 / math.sqrt(channels))
        token_cols[...] = noised.astype(BF16)
        token_rows[...] = noised.T.astype(BF16)
        target[...] = (draw - latent).T
        order = lax.broadcasted_iota(jnp.int32, (half_width, tokens), 0).astype(F32)
        angles = (1000.0 * level) * jnp.exp(-math.log(10000.0) * order / half_width)
        root = 1.0 / math.sqrt(2 * half_width)
        for part, wave in enumerate((jnp.cos(angles), jnp.sin(angles))):
            wave = wave.astype(BF16).astype(F32) * root
            place = pl.ds(part * half_width, half_width)
            embed_cols[place, :] = wave.astype(BF16)
            embed_rows[:, place] = wave.T.astype(BF16)
    rows = modulation[fragment[0]]
    half = rows.shape[1] // CORES
    for side in range(CORES):
        factor, shift, terms = outs[per_step * steps + 3 * side : per_step * steps + 3 * (side + 1)]

        def place_half(first):
            here = rows[:, first : first + half]
            factor[...] = 1.0 + here[1:2]
            shift[...] = here[0:1]
            wide = jnp.broadcast_to(here[0:1], terms.shape)
            high = wide.astype(BF16).astype(F32)
            index = lax.broadcasted_iota(jnp.int32, terms.shape, 0)
            split = jnp.where(index == 0, high, jnp.where(index == 1, wide - high, 0.0))
            terms[...] = split.astype(BF16)

        @pl.when(core[0] == side)
        def _():
            place_half(0)

        @pl.when(core[0] != side)
        def _():
            place_half(half)


def prepare(core, fragment, latents, noise_draw, timesteps, modulation, time_width):
    steps, tokens, channels = latents.shape
    half = modulation.shape[2] // CORES
    outs = [
        ((tokens, channels), BF16),
        ((tokens, time_width), BF16),
        ((channels, tokens), BF16),
        ((time_width, tokens), BF16),
        ((tokens, channels), F32),
    ] * steps + [((1, half), F32), ((1, half), F32), ((16, half), BF16)] * CORES
    args = (latents.transpose(0, 2, 1), noise_draw.transpose(0, 2, 1), timesteps, modulation)
    results = local_call(
        prepare_kernel, "prepare", args, outs, scalars=(core, fragment), flops=2**32
    )
    return [results[5 * s : 5 * s + 5] for s in range(steps)], [
        results[5 * steps + 3 * c : 5 * steps + 3 * c + 3] for c in range(CORES)
    ]


def pair_sum_kernel(mine, got, out):
    out[...] = (mine[...].astype(F32) + got[...].astype(F32)).astype(BF16)


def step_kernel(blocks, params, mean, square, new_mean, new_square, new_params, copies):
    first, second, new = adam(blocks, params, mean, square)
    new_mean[...] = first
    new_square[...] = second
    new_params[...] = new
    block = new.astype(BF16)
    for chip in range(copies.shape[0]):
        copies[chip] = block


def last_kernel(blocks, params, mean, square, start, new_mean, new_square, strips):
    first, second, new = adam(blocks, params, mean, square)
    new_mean[...] = first
    new_square[...] = second
    drift = (start[...] - new).astype(BF16)
    rows, columns = strips.shape[1:]
    used = 0
    for top in range(0, drift.shape[0], rows):
        for left in range(0, drift.shape[1], columns):
            strips[used] = drift[top : top + rows, left : left + columns]
            used += 1
    for index in range(used, strips.shape[0]):
        strips[index] = jnp.zeros((rows, columns), BF16)


def adam(blocks, params, mean, square):
    gradient = blocks[0].astype(F32)
    for chip in range(1, blocks.shape[0]):
        gradient = gradient + blocks[chip].astype(F32)
    old = params[...]
    first = BETA_ONE * mean[...] + (1.0 - BETA_ONE) * gradient
    second = BETA_TWO * square[...] + (1.0 - BETA_TWO) * gradient * gradient
    new = old - INNER_RATE * (first / (jnp.sqrt(second) + ADAM_EPS) + DECAY_RATE * old)
    return first, second, new


def strip_sum_kernel(strips, copies):
    total = strips[0].astype(F32)
    for index in range(1, strips.shape[0]):
        total = total + strips[index].astype(F32)
    block = total.astype(BF16)
    for index in range(copies.shape[0]):
        copies[index] = block


def make_outer_kernel(replicas):
    def outer_kernel(core, own, got, params, momentum, new_params, new_momentum, own_buf, got_buf):
        strip_rows, strip_columns = own.shape[1:]
        rows = params.shape[0]
        half = params.shape[1] // CORES
        index = 0
        for top in range(0, rows * CORES, strip_rows):
            for left in range(0, half, strip_columns):
                place = (slice(top, top + strip_rows), slice(left, left + strip_columns))
                own_buf[place] = own[index].astype(F32)
                got_buf[place] = got[index].astype(F32)
                index += 1

        def finish(cols, values):
            average = values * (1.0 / replicas)
            moved = NESTEROV * momentum[:, cols] + average
            new_momentum[:, cols] = moved
            new_params[:, cols] = params[:, cols] - OUTER_RATE * (average + NESTEROV * moved)

        @pl.when(core[0] == 0)
        def _():
            finish(slice(0, half), own_buf[0:rows])
            finish(slice(half, 2 * half), got_buf[0:rows])

        @pl.when(core[0] != 0)
        def _():
            finish(slice(0, half), got_buf[rows:])
            finish(slice(half, 2 * half), own_buf[rows:])

    return outer_kernel


def on_device(
    outer_params,
    outer_momentum,
    inner_mean,
    inner_square,
    latents,
    noise_draw,
    timesteps,
    fragment,
    modulation,
):
    width = lax.axis_size("fsdp")
    replicas = lax.axis_size("replica")
    chips = width // CORES
    core = (lax.axis_index("fsdp") % CORES).astype(jnp.int32)
    core_arg = core.reshape(1)
    rows, model_width = outer_params.shape
    half = model_width // CORES
    channels = latents.shape[2]
    time_width = rows * width - 2 * channels
    total_rows = latents.shape[1] * width

    pair_shape = (rows * CORES, half)
    start, copies = local_call(
        start_kernel,
        "start",
        (hold(outer_params), core_swap(outer_params, width)),
        [(pair_shape, F32), ((chips,) + pair_shape, BF16)],
        scalars=(core_arg,),
    )
    gathered = chip_exchange(copies, width)

    prepared, mods = prepare(
        core_arg, fragment, latents, noise_draw, timesteps, modulation, time_width
    )
    params = start
    mean, square = local_call(
        moments_kernel,
        "moments",
        (
            inner_mean[0],
            core_swap(inner_mean[0], width),
            inner_square[0],
            core_swap(inner_square[0], width),
        ),
        [(pair_shape, F32)] * 2,
        scalars=(core_arg,),
    )
    gathered, prepared, mods, mean, square = lax.optimization_barrier(
        (gathered, prepared, mods, mean, square)
    )

    for step in range(STEPS):
        tokens, embed, tokens_t, embed_t, target = prepared[step]
        weights = gathered.reshape(chips * pair_shape[0], half)
        other = core_swap(weights, width)
        state = forward(tokens, embed, weights, mods[0][0], mods[0][2])
        state_other = forward(tokens, embed, other, mods[1][0], mods[1][2])
        shapes = [
            ((target.shape[0], channels), BF16),
            ((channels, target.shape[0]), BF16),
            ((target.shape[0], LANES), F32),
            ((channels, LANES), F32),
        ]
        head = local_call(
            make_head_kernel(model_width, total_rows),
            "head",
            (state[3], state_other[3], state[4], state_other[4], state[5], state_other[5], target),
            shapes,
        )
        grad_other = backward(
            state_other[:3], other, mods[1][0], mods[1][1], tokens_t, embed_t, head, model_width
        )
        received = core_swap(grad_other, width)
        head, grad_other = lax.optimization_barrier((head, grad_other))
        grad_mine = backward(
            state[:3], weights, mods[0][0], mods[0][1], tokens_t, embed_t, head, model_width
        )
        pair_sum = local_call(
            pair_sum_kernel, "pair_sum", (grad_mine, received), [(weights.shape, BF16)]
        )[0]
        blocks = chip_exchange(pair_sum.reshape((chips,) + pair_shape), width)
        moments = [(pair_shape, F32)] * 2
        if step + 1 < STEPS:
            outs = moments + [(pair_shape, F32), ((chips,) + pair_shape, BF16)]
            mean, square, params, copies = local_call(
                step_kernel, "update", (blocks, params, mean, square), outs
            )
            gathered = chip_exchange(copies, width)
        else:
            strip = (STRIP_ROWS, half // STRIP_PARTS)
            outs = moments + [((replicas,) + strip, BF16)]
            mean, square, strips = local_call(
                last_kernel, "update_last", (blocks, params, mean, square, start), outs
            )
    strips = lax.all_to_all(strips, "replica", 0, 0)
    new_mean, new_square = local_call(
        unpair_kernel,
        "unpair",
        (mean, core_swap(mean, width), square, core_swap(square, width)),
        [(outer_params.shape, F32)] * 2,
        scalars=(core_arg,),
        hbm_outs=True,
    )
    strips, new_mean, new_square = lax.optimization_barrier((strips, new_mean, new_square))
    strips = local_call(strip_sum_kernel, "strip_sum", (strips,), [(strips.shape, BF16)])[0]
    strips = lax.all_to_all(strips, "replica", 0, 0)
    new_params, new_momentum = local_call(
        make_outer_kernel(replicas),
        "outer",
        (strips, core_swap(strips, width), outer_params, outer_momentum),
        [(outer_params.shape, F32)] * 2,
        [pltpu.VMEM(pair_shape, F32)] * 2,
        scalars=(core_arg,),
        hbm_outs=True,
    )
    return (new_params, new_momentum, new_mean[None], new_square[None])


def solution(mesh):
    return jax.shard_map(
        on_device,
        mesh=mesh,
        in_specs=(
            P("fsdp", None),
            P("fsdp", None),
            P("replica", "fsdp", None),
            P("replica", "fsdp", None),
            P(None, ("replica", "fsdp"), None),
            P(None, ("replica", "fsdp"), None),
            P(None, ("replica", "fsdp")),
            P(),
            P(),
        ),
        out_specs=(
            P("fsdp", None),
            P("fsdp", None),
            P("replica", "fsdp", None),
            P("replica", "fsdp", None),
        ),
        check_vma=False,
    )
```

```python
import math

import jax
import jax.numpy as jnp
from jax import lax
from jax.experimental import pallas as pl
from jax.experimental.pallas import tpu as pltpu
from jax.sharding import PartitionSpec as P

STEPS = 2
LEVELS = 1000


BETA_ONE = 0.9
BETA_TWO = 0.95
INNER_RATE = 0.2
DECAY_RATE = 0.1
ADAM_EPS = 1e-08
NORM_EPS = 1e-06
OUTER_RATE = 0.7
NESTEROV = 0.9

CORES = 2
LANES = 128
ROW_CHUNK = 16
FWD_COLUMNS = 256
STRIP_ROWS = 16
STRIP_PARTS = 4
KERNEL_VMEM = 24 * 2**20

BF16 = jnp.bfloat16
F32 = jnp.float32
VMEM = pl.BlockSpec(memory_space=pltpu.VMEM)
SMEM = pl.BlockSpec(memory_space=pltpu.SMEM)
TRANSPOSED = (((1,), (1,)), ((), ()))


def local_call(kernel, name, args, outs, scratch=(), scalars=(), flops=0, hbm_outs=False):
    place = pltpu.VMEM if not hbm_outs else jax.ShapeDtypeStruct
    specs = [SMEM] * len(scalars) + [VMEM] * len(args)
    values = [*scalars, *(pltpu.with_memory_space_constraint(a, pltpu.VMEM) for a in args)]
    moved = sum(math.prod(o[0]) * 4 for o in outs) + sum(a.size * a.dtype.itemsize for a in args)
    return pl.pallas_call(
        kernel,
        in_specs=specs,
        out_specs=[VMEM] * len(outs),
        out_shape=[place(shape, dtype) for shape, dtype in outs],
        scratch_shapes=list(scratch),
        compiler_params=pltpu.CompilerParams(vmem_limit_bytes=KERNEL_VMEM),
        cost_estimate=pl.CostEstimate(flops=flops, bytes_accessed=moved, transcendentals=0),
        name=name,
    )(*values)


def core_swap(values, width):
    return lax.ppermute(values, "fsdp", [(i, i ^ 1) for i in range(width)])


def chip_exchange(blocks, width):
    groups = [list(range(core, width, CORES)) for core in range(CORES)]
    return lax.all_to_all(blocks, "fsdp", 0, 0, axis_index_groups=groups)


def hold_kernel(values, held):
    held[...] = values[...]


def hold(values):
    return local_call(hold_kernel, "hold", (values,), [(values.shape, values.dtype)])[0]


def pair_halves(core, own, got, pair):
    rows = own.shape[0]
    half = own.shape[1] // CORES

    @pl.when(core[0] == 0)
    def _():
        pair[0:rows] = own[:, 0:half]
        pair[rows:] = got[:, 0:half]

    @pl.when(core[0] != 0)
    def _():
        pair[0:rows] = got[:, half:]
        pair[rows:] = own[:, half:]


def start_kernel(core, own, got, pair, copies):
    pair_halves(core, own, got, pair)
    block = pair[...].astype(BF16)
    for chip in range(copies.shape[0]):
        copies[chip] = block


def moments_kernel(core, mean, mean_got, square, square_got, mean_pair, square_pair):
    pair_halves(core, mean, mean_got, mean_pair)
    pair_halves(core, square, square_got, square_pair)


def unpair_halves(core, own, got, out):
    rows = out.shape[0]
    half = out.shape[1] // CORES

    @pl.when(core[0] == 0)
    def _():
        out[:, 0:half] = own[0:rows]
        out[:, half:] = got[0:rows]

    @pl.when(core[0] != 0)
    def _():
        out[:, 0:half] = got[rows:]
        out[:, half:] = own[rows:]


def unpair_kernel(core, mean, mean_got, square, square_got, new_mean, new_square):
    unpair_halves(core, mean, mean_got, new_mean)
    unpair_halves(core, square, square_got, new_square)


def scaled_out_weight(weights, factor, time_end):
    return (weights[time_end:, :].astype(F32) * factor[0:1, :]).astype(BF16)


def forward_kernel(tokens, embed, weights, factor, shift, hid, slope, stats, pre_buf, in_buf, square):
    rows_here, channels = tokens.shape
    time_end = channels + embed.shape[1]
    square[...] = jnp.zeros_like(square)
    for index in range(weights.shape[1] // FWD_COLUMNS):
        slot = index % 2
        cols = pl.ds(index * FWD_COLUMNS, FWD_COLUMNS)
        pre_buf[slot] = jnp.dot(
            embed[...], weights[channels:time_end, cols], preferred_element_type=F32
        )
        in_buf[slot] = jnp.dot(tokens[...], weights[0:channels, cols], preferred_element_type=F32)
        for start in range(0, rows_here, ROW_CHUNK):
            rows = pl.ds(start, ROW_CHUNK)
            half_pre = pre_buf[slot, rows, :]
            wave = jnp.tanh(half_pre)
            above = wave + 1.0
            silu = half_pre * above
            hidden = in_buf[slot, rows, :] + silu
            hid[rows, cols] = hidden.astype(BF16)
            slope[rows, cols] = (above + silu * (1.0 - wave)).astype(BF16)
            power = hidden * hidden
            partial = power[:, 0:LANES]
            for lane in range(LANES, FWD_COLUMNS, LANES):
                partial = partial + power[:, lane : lane + LANES]
            square[rows, :] += partial
    scaled = scaled_out_weight(weights, factor, time_end)
    out = lax.dot_general(hid[...], scaled, TRANSPOSED, preferred_element_type=F32)
    bias = lax.dot_general(
        shift[...], weights[time_end:, :], TRANSPOSED, preferred_element_type=F32
    )
    power = jnp.sum(square[...], axis=1, keepdims=True)
    stats[0:rows_here, :] = jnp.concatenate(
        [out, jnp.broadcast_to(power, (rows_here, LANES - channels))], axis=1
    )
    stats[rows_here:, :] = jnp.concatenate([bias, jnp.zeros_like(bias)], axis=1)


def forward(tokens, embed, weights, factor, shift):
    rows, columns = tokens.shape[0], weights.shape[1]
    outs = [((rows, columns), BF16)] * 2 + [((rows + shift.shape[0], LANES), F32)]
    scratch = [pltpu.VMEM((2, rows, FWD_COLUMNS), F32)] * 2 + [pltpu.VMEM((rows, LANES), F32)]
    flops = 2 * rows * columns * weights.shape[0]
    args = (tokens, embed, weights, factor, shift)
    return local_call(forward_kernel, "forward", args, outs, scratch, flops=flops)


def make_backward_kernel(model_width, total_rows, added):
    def backward_kernel(
        own, got, target, hid, slope, weights, factor, shift, tokens_t, embed_t, *rest
    ):
        before = rest[0] if added else None
        out, mod_buf, hid_buf, pre_buf, pull = rest[1:] if added else rest
        root = 1.0 / math.sqrt(model_width)
        rows_here, channels = target.shape
        time_end = channels + embed_t.shape[0]
        columns = out.shape[1]

        both = own[0:rows_here, :] + got[0:rows_here, :]
        raw = both[:, 0:channels]
        inverse = lax.rsqrt(both[:, channels : channels + 1] * (1.0 / model_width) + NORM_EPS)
        terms = own[rows_here:, 0:channels] + got[rows_here:, 0:channels]
        bias = jnp.sum(terms, axis=0, keepdims=True)
        output = (inverse * raw + bias) * root
        out_grad = (2.0 / (total_rows * channels)) * (output - target[...])
        grad = (out_grad * (inverse * root)).astype(BF16)
        wide = grad.astype(F32)
        grad_t = wide.T.astype(BF16)
        pulled = inverse * inverse * (1.0 / model_width)
        pulled = pulled * jnp.sum(wide * raw, axis=1, keepdims=True)
        pull[...] = jnp.broadcast_to(pulled, pull.shape)
        grad_sum = jnp.sum(out_grad.T, axis=1, keepdims=True) * root

        scaled = scaled_out_weight(weights, factor, time_end)
        mod_buf[...] = jnp.dot(grad, scaled, preferred_element_type=F32)
        for start in range(0, rows_here, ROW_CHUNK):
            rows = pl.ds(start, ROW_CHUNK)
            spread = jnp.concatenate([pull[rows, :]] * (columns // LANES), axis=1)
            hid_grad = mod_buf[rows, :] - hid[rows, :].astype(F32) * spread
            hid_buf[rows, :] = hid_grad.astype(BF16)
            pre_buf[rows, :] = (hid_grad * slope[rows, :].astype(F32)).astype(BF16)

        def put(rows, values):
            if added:
                values = values + before[rows, :]
            out[rows, :] = values.astype(out.dtype)

        put(
            slice(0, channels),
            jnp.dot(tokens_t[...], hid_buf[...], preferred_element_type=F32),
        )
        put(
            slice(channels, time_end),
            jnp.dot(embed_t[...], pre_buf[...], preferred_element_type=F32),
        )
        grad_out = jnp.dot(grad_t, hid[...], preferred_element_type=F32)
        put(
            slice(time_end, out.shape[0]),
            grad_out * factor[0:1, :] + grad_sum * shift[0:1, :],
        )

    return backward_kernel


def backward(stats, target, state, weights, factor, shift, tokens_t, embed_t, before, sizes):
    rows, columns = state[0].shape
    scratch = [
        pltpu.VMEM((rows, columns), F32),
        pltpu.VMEM((rows, columns), BF16),
        pltpu.VMEM((rows, columns), BF16),
        pltpu.VMEM((rows, LANES), F32),
    ]
    flops = 2 * rows * columns * (weights.shape[0] + tokens_t.shape[0])
    args = (*stats, target, *state, weights, factor, shift, tokens_t, embed_t, *before)
    outs = [(weights.shape, BF16 if before else F32)]
    kernel = make_backward_kernel(*sizes, bool(before))
    return local_call(kernel, "backward", args, outs, scratch, flops=flops)[0]


def prepare_kernel(
    core, fragment, latents, latents_got, noise, noise_got, levels, levels_got, modulation, *rest
):
    outs, (latent_buf, noise_buf, level_buf) = rest[:-3], rest[-3:]
    steps, channels, tokens = latents.shape
    half_width = outs[1].shape[1] // 2
    pairs = ((latents, latents_got), (noise, noise_got), (levels, levels_got))
    for buffer, (own, got) in zip((latent_buf, noise_buf, level_buf), pairs):

        @pl.when(core[0] == 0)
        def _():
            buffer[0] = own[...]
            buffer[1] = got[...]

        @pl.when(core[0] != 0)
        def _():
            buffer[0] = got[...]
            buffer[1] = own[...]

    place = 0
    for step in range(steps):
        for owner in range(CORES):
            token_rows, embed_rows, token_cols, embed_cols, target = outs[place : place + 5]
            place += 5
            level = (level_buf[owner, step : step + 1, :].astype(F32) + 0.5) / LEVELS
            latent = latent_buf[owner, step].astype(F32)
            draw = noise_buf[owner, step].astype(F32)
            noised = ((1.0 - level) * latent + level * draw).astype(BF16).astype(F32)
            noised = noised * (1.0 / math.sqrt(channels))
            token_cols[...] = noised.astype(BF16)
            token_rows[...] = noised.T.astype(BF16)
            target[...] = (draw - latent).T
            order = lax.broadcasted_iota(jnp.int32, (half_width, tokens), 0).astype(F32)
            angles = (1000.0 * level) * jnp.exp(-math.log(10000.0) * order / half_width)
            root = 0.5 / math.sqrt(2 * half_width)
            for part, wave in enumerate((jnp.cos(angles), jnp.sin(angles))):
                wave = wave.astype(BF16).astype(F32) * root
                here = pl.ds(part * half_width, half_width)
                embed_cols[here, :] = wave.astype(BF16)
                embed_rows[:, here] = wave.T.astype(BF16)
    rows = modulation[fragment[0]]
    half = rows.shape[1] // CORES
    factor, shift, terms = outs[place:]

    for side in range(CORES):

        @pl.when(core[0] == side)
        def _():
            here = rows[:, side * half : (side + 1) * half]
            factor[...] = 1.0 + here[1:2]
            shift[...] = here[0:1]
            wide = jnp.broadcast_to(here[0:1], terms.shape)
            high = wide.astype(BF16).astype(F32)
            index = lax.broadcasted_iota(jnp.int32, terms.shape, 0)
            split = jnp.where(index == 0, high, jnp.where(index == 1, wide - high, 0.0))
            terms[...] = split.astype(BF16)


def prepare(core, fragment, latents, noise_draw, timesteps, modulation, time_width, width):
    steps, tokens, channels = latents.shape
    half = modulation.shape[2] // CORES
    outs = [
        ((tokens, channels), BF16),
        ((tokens, time_width), BF16),
        ((channels, tokens), BF16),
        ((time_width, tokens), BF16),
        ((tokens, channels), F32),
    ] * (steps * CORES) + [((1, half), F32), ((1, half), F32), ((16, half), BF16)]
    args = []
    scratch = []
    for values in (latents.transpose(0, 2, 1), noise_draw.transpose(0, 2, 1), timesteps):
        args += [values, core_swap(values, width)]
        scratch.append(pltpu.VMEM((CORES,) + values.shape, values.dtype))
    results = local_call(
        prepare_kernel,
        "prepare",
        (*args, modulation),
        outs,
        scratch,
        scalars=(core, fragment),
        flops=2**32,
    )
    sets = [results[5 * i : 5 * i + 5] for i in range(steps * CORES)]
    return [sets[CORES * s : CORES * (s + 1)] for s in range(steps)], results[-3:]


def step_kernel(blocks, params, mean, square, new_mean, new_square, new_params, copies):
    first, second, new = adam(blocks, params, mean, square)
    new_mean[...] = first
    new_square[...] = second
    new_params[...] = new
    block = new.astype(BF16)
    for chip in range(copies.shape[0]):
        copies[chip] = block


def last_kernel(blocks, params, mean, square, start, new_mean, new_square, strips):
    first, second, new = adam(blocks, params, mean, square)
    new_mean[...] = first
    new_square[...] = second
    drift = (start[...] - new).astype(BF16)
    rows, columns = strips.shape[1:]
    used = 0
    for top in range(0, drift.shape[0], rows):
        for left in range(0, drift.shape[1], columns):
            strips[used] = drift[top : top + rows, left : left + columns]
            used += 1
    for index in range(used, strips.shape[0]):
        strips[index] = jnp.zeros((rows, columns), BF16)


def adam(blocks, params, mean, square):
    gradient = blocks[0].astype(F32)
    for chip in range(1, blocks.shape[0]):
        gradient = gradient + blocks[chip].astype(F32)
    old = params[...]
    first = BETA_ONE * mean[...] + (1.0 - BETA_ONE) * gradient
    second = BETA_TWO * square[...] + (1.0 - BETA_TWO) * gradient * gradient
    new = old - INNER_RATE * (first / (jnp.sqrt(second) + ADAM_EPS) + DECAY_RATE * old)
    return first, second, new


def strip_sum_kernel(strips, copies):
    total = strips[0].astype(F32)
    for index in range(1, strips.shape[0]):
        total = total + strips[index].astype(F32)
    block = total.astype(BF16)
    for index in range(copies.shape[0]):
        copies[index] = block


def make_outer_kernel(replicas):
    def outer_kernel(core, own, got, params, momentum, new_params, new_momentum, own_buf, got_buf):
        strip_rows, strip_columns = own.shape[1:]
        rows = params.shape[0]
        half = params.shape[1] // CORES
        index = 0
        for top in range(0, rows * CORES, strip_rows):
            for left in range(0, half, strip_columns):
                place = (slice(top, top + strip_rows), slice(left, left + strip_columns))
                own_buf[place] = own[index].astype(F32)
                got_buf[place] = got[index].astype(F32)
                index += 1

        def finish(cols, values):
            average = values * (1.0 / replicas)
            moved = NESTEROV * momentum[:, cols] + average
            new_momentum[:, cols] = moved
            new_params[:, cols] = params[:, cols] - OUTER_RATE * (average + NESTEROV * moved)

        @pl.when(core[0] == 0)
        def _():
            finish(slice(0, half), own_buf[0:rows])
            finish(slice(half, 2 * half), got_buf[0:rows])

        @pl.when(core[0] != 0)
        def _():
            finish(slice(0, half), got_buf[rows:])
            finish(slice(half, 2 * half), own_buf[rows:])

    return outer_kernel


def on_device(
    outer_params,
    outer_momentum,
    inner_mean,
    inner_square,
    latents,
    noise_draw,
    timesteps,
    fragment,
    modulation,
):
    width = lax.axis_size("fsdp")
    replicas = lax.axis_size("replica")
    chips = width // CORES
    core = (lax.axis_index("fsdp") % CORES).astype(jnp.int32)
    core_arg = core.reshape(1)
    rows, model_width = outer_params.shape
    half = model_width // CORES
    channels = latents.shape[2]
    time_width = rows * width - 2 * channels
    total_rows = latents.shape[1] * width

    pair_shape = (rows * CORES, half)
    start, copies = local_call(
        start_kernel,
        "start",
        (hold(outer_params), core_swap(outer_params, width)),
        [(pair_shape, F32), ((chips,) + pair_shape, BF16)],
        scalars=(core_arg,),
    )
    gathered = chip_exchange(copies, width)

    prepared, mods = prepare(
        core_arg, fragment, latents, noise_draw, timesteps, modulation, time_width, width
    )
    params = start
    mean, square = local_call(
        moments_kernel,
        "moments",
        (
            inner_mean[0],
            core_swap(inner_mean[0], width),
            inner_square[0],
            core_swap(inner_square[0], width),
        ),
        [(pair_shape, F32)] * 2,
        scalars=(core_arg,),
    )
    gathered, prepared, mods, mean, square = lax.optimization_barrier(
        (gathered, prepared, mods, mean, square)
    )

    sizes = (model_width, total_rows)
    factor, shift, terms = mods
    for step in range(STEPS):
        weights = gathered.reshape(chips * pair_shape[0], half)
        states = []
        for tokens, embed, _, _, _ in prepared[step]:
            hid, slope, stats = forward(tokens, embed, weights, factor, terms)
            states.append(((hid, slope), (stats, core_swap(stats, width))))
        gradient = ()
        for (state, stats), (_, _, tokens_t, embed_t, target) in zip(states, prepared[step]):
            gradient = (
                backward(
                    stats, target, state, weights, factor, shift, tokens_t, embed_t, gradient, sizes
                ),
            )
        pair_sum = gradient[0]
        blocks = chip_exchange(pair_sum.reshape((chips,) + pair_shape), width)
        moments = [(pair_shape, F32)] * 2
        if step + 1 < STEPS:
            outs = moments + [(pair_shape, F32), ((chips,) + pair_shape, BF16)]
            mean, square, params, copies = local_call(
                step_kernel, "update", (blocks, params, mean, square), outs
            )
            gathered = chip_exchange(copies, width)
        else:
            strip = (STRIP_ROWS, half // STRIP_PARTS)
            outs = moments + [((replicas,) + strip, BF16)]
            mean, square, strips = local_call(
                last_kernel, "update_last", (blocks, params, mean, square, start), outs
            )
    strips = lax.all_to_all(strips, "replica", 0, 0)
    new_mean, new_square = local_call(
        unpair_kernel,
        "unpair",
        (mean, core_swap(mean, width), square, core_swap(square, width)),
        [(outer_params.shape, F32)] * 2,
        scalars=(core_arg,),
        hbm_outs=True,
    )
    strips, new_mean, new_square = lax.optimization_barrier((strips, new_mean, new_square))
    strips = local_call(strip_sum_kernel, "strip_sum", (strips,), [(strips.shape, BF16)])[0]
    strips = lax.all_to_all(strips, "replica", 0, 0)
    new_params, new_momentum = local_call(
        make_outer_kernel(replicas),
        "outer",
        (strips, core_swap(strips, width), outer_params, outer_momentum),
        [(outer_params.shape, F32)] * 2,
        [pltpu.VMEM(pair_shape, F32)] * 2,
        scalars=(core_arg,),
        hbm_outs=True,
    )
    return (new_params, new_momentum, new_mean[None], new_square[None])


def solution(mesh):
    return jax.shard_map(
        on_device,
        mesh=mesh,
        in_specs=(
            P("fsdp", None),
            P("fsdp", None),
            P("replica", "fsdp", None),
            P("replica", "fsdp", None),
            P(None, ("replica", "fsdp"), None),
            P(None, ("replica", "fsdp"), None),
            P(None, ("replica", "fsdp")),
            P(),
            P(),
        ),
        out_specs=(
            P("fsdp", None),
            P("fsdp", None),
            P("replica", "fsdp", None),
            P("replica", "fsdp", None),
        ),
        check_vma=False,
    )
```

```python
import math

import jax
import jax.numpy as jnp
from jax import lax
from jax.experimental import pallas as pl
from jax.experimental.pallas import tpu as pltpu
from jax.sharding import PartitionSpec as P

STEPS = 2
LEVELS = 1000


BETA_ONE = 0.9
BETA_TWO = 0.95
INNER_RATE = 0.2
DECAY_RATE = 0.1
ADAM_EPS = 1e-08
NORM_EPS = 1e-06
OUTER_RATE = 0.7
NESTEROV = 0.9

CORES = 2
LANES = 128
ROW_CHUNK = 16
FWD_COLUMNS = 256
STRIP_ROWS = 16
STRIP_PARTS = 4
KERNEL_VMEM = 24 * 2**20

BF16 = jnp.bfloat16
F32 = jnp.float32
VMEM = pl.BlockSpec(memory_space=pltpu.VMEM)
SMEM = pl.BlockSpec(memory_space=pltpu.SMEM)
TRANSPOSED = (((1,), (1,)), ((), ()))
BOTH_TRANSPOSED = (((0,), (0,)), ((), ()))


def local_call(kernel, name, args, outs, scratch=(), scalars=(), flops=0, hbm_outs=False):
    place = pltpu.VMEM if not hbm_outs else jax.ShapeDtypeStruct
    specs = [SMEM] * len(scalars) + [VMEM] * len(args)
    values = [*scalars, *(pltpu.with_memory_space_constraint(a, pltpu.VMEM) for a in args)]
    moved = sum(math.prod(o[0]) * 4 for o in outs) + sum(a.size * a.dtype.itemsize for a in args)
    return pl.pallas_call(
        kernel,
        in_specs=specs,
        out_specs=[VMEM] * len(outs),
        out_shape=[place(shape, dtype) for shape, dtype in outs],
        scratch_shapes=list(scratch),
        compiler_params=pltpu.CompilerParams(vmem_limit_bytes=KERNEL_VMEM),
        cost_estimate=pl.CostEstimate(flops=flops, bytes_accessed=moved, transcendentals=0),
        name=name,
    )(*values)


def core_swap(values, width):
    return lax.ppermute(values, "fsdp", [(i, i ^ 1) for i in range(width)])


def chip_exchange(blocks, width):
    groups = [list(range(core, width, CORES)) for core in range(CORES)]
    return lax.all_to_all(blocks, "fsdp", 0, 0, axis_index_groups=groups)


def hold_kernel(values, held):
    held[...] = values[...]


def hold(values):
    return local_call(hold_kernel, "hold", (values,), [(values.shape, values.dtype)])[0]


def pair_halves(core, own, got, pair):
    rows = own.shape[0]
    half = own.shape[1] // CORES

    @pl.when(core[0] == 0)
    def _():
        pair[0:rows] = own[:, 0:half]
        pair[rows:] = got[:, 0:half]

    @pl.when(core[0] != 0)
    def _():
        pair[0:rows] = got[:, half:]
        pair[rows:] = own[:, half:]


def start_kernel(core, own, got, pair, copies):
    pair_halves(core, own, got, pair)
    block = pair[...].astype(BF16)
    for chip in range(copies.shape[0]):
        copies[chip] = block


def moments_kernel(core, mean, mean_got, square, square_got, mean_pair, square_pair):
    pair_halves(core, mean, mean_got, mean_pair)
    pair_halves(core, square, square_got, square_pair)


def unpair_halves(core, own, got, out):
    rows = out.shape[0]
    half = out.shape[1] // CORES

    @pl.when(core[0] == 0)
    def _():
        out[:, 0:half] = own[0:rows]
        out[:, half:] = got[0:rows]

    @pl.when(core[0] != 0)
    def _():
        out[:, 0:half] = got[rows:]
        out[:, half:] = own[rows:]


def unpair_kernel(core, mean, mean_got, square, square_got, new_mean, new_square):
    unpair_halves(core, mean, mean_got, new_mean)
    unpair_halves(core, square, square_got, new_square)


def scaled_out_weight(weights, factor, time_end):
    return (weights[time_end:, :].astype(F32) * factor[0:1, :]).astype(BF16)


def forward_kernel(inputs_t, weights, factor, shift, hid, slope, stats, pre_buf, in_buf, square):
    time_end, rows_here = inputs_t.shape
    channels = weights.shape[0] - time_end
    square[...] = jnp.zeros_like(square)
    for index in range(weights.shape[1] // FWD_COLUMNS):
        slot = index % 2
        cols = pl.ds(index * FWD_COLUMNS, FWD_COLUMNS)
        pre_buf[slot] = lax.dot_general(
            inputs_t[channels:, :],
            weights[channels:time_end, cols],
            BOTH_TRANSPOSED,
            preferred_element_type=F32,
        )
        in_buf[slot] = lax.dot_general(
            inputs_t[0:channels, :],
            weights[0:channels, cols],
            BOTH_TRANSPOSED,
            preferred_element_type=F32,
        )
        for start in range(0, rows_here, ROW_CHUNK):
            rows = pl.ds(start, ROW_CHUNK)
            half_pre = pre_buf[slot, rows, :]
            wave = jnp.tanh(half_pre)
            above = wave + 1.0
            silu = half_pre * above
            hidden = in_buf[slot, rows, :] + silu
            hid[rows, cols] = hidden.astype(BF16)
            slope[rows, cols] = (above + silu * (1.0 - wave)).astype(BF16)
            power = hidden * hidden
            partial = power[:, 0:LANES]
            for lane in range(LANES, FWD_COLUMNS, LANES):
                partial = partial + power[:, lane : lane + LANES]
            square[rows, :] += partial
    scaled = scaled_out_weight(weights, factor, time_end)
    out = lax.dot_general(hid[...], scaled, TRANSPOSED, preferred_element_type=F32)
    bias = lax.dot_general(
        shift[...], weights[time_end:, :], TRANSPOSED, preferred_element_type=F32
    )
    power = jnp.sum(square[...], axis=1, keepdims=True)
    stats[0:rows_here, :] = jnp.concatenate(
        [out, jnp.broadcast_to(power, (rows_here, LANES - channels))], axis=1
    )
    stats[rows_here:, :] = jnp.concatenate([bias, jnp.zeros_like(bias)], axis=1)


def forward(inputs_t, weights, factor, shift):
    rows, columns = inputs_t.shape[1], weights.shape[1]
    outs = [((rows, columns), BF16)] * 2 + [((rows + shift.shape[0], LANES), F32)]
    scratch = [pltpu.VMEM((2, rows, FWD_COLUMNS), F32)] * 2 + [pltpu.VMEM((rows, LANES), F32)]
    flops = 2 * rows * columns * weights.shape[0]
    args = (inputs_t, weights, factor, shift)
    return local_call(forward_kernel, "forward", args, outs, scratch, flops=flops)


def make_backward_kernel(model_width, total_rows, added):
    def backward_kernel(
        own, got, target_t, hid, slope, weights, factor, shift, inputs_t, *rest
    ):
        before = rest[0] if added else None
        out, mod_buf, hid_buf, pre_buf, pull = rest[1:] if added else rest
        root = 1.0 / math.sqrt(model_width)
        channels, rows_here = target_t.shape
        time_end = inputs_t.shape[0]
        columns = out.shape[1]

        both = own[0:rows_here, :] + got[0:rows_here, :]
        raw = both[:, 0:channels]
        inverse = lax.rsqrt(both[:, channels : channels + 1] * (1.0 / model_width) + NORM_EPS)
        terms = own[rows_here:, 0:channels] + got[rows_here:, 0:channels]
        bias = jnp.sum(terms, axis=0, keepdims=True)
        output = (inverse * raw + bias) * root
        out_grad = (2.0 / (total_rows * channels)) * (output - target_t[...].T)
        grad = (out_grad * (inverse * root)).astype(BF16)
        wide = grad.astype(F32)
        grad_t = wide.T.astype(BF16)
        pulled = inverse * inverse * (1.0 / model_width)
        pulled = pulled * jnp.sum(wide * raw, axis=1, keepdims=True)
        pull[...] = jnp.broadcast_to(pulled, pull.shape)
        grad_sum = jnp.sum(out_grad.T, axis=1, keepdims=True) * root

        scaled = scaled_out_weight(weights, factor, time_end)
        mod_buf[...] = jnp.dot(grad, scaled, preferred_element_type=F32)
        for start in range(0, rows_here, ROW_CHUNK):
            rows = pl.ds(start, ROW_CHUNK)
            spread = jnp.concatenate([pull[rows, :]] * (columns // LANES), axis=1)
            hid_grad = mod_buf[rows, :] - hid[rows, :].astype(F32) * spread
            hid_buf[rows, :] = hid_grad.astype(BF16)
            pre_buf[rows, :] = (hid_grad * slope[rows, :].astype(F32)).astype(BF16)

        def put(rows, values):
            if added:
                values = values + before[rows, :]
            out[rows, :] = values.astype(out.dtype)

        put(
            slice(0, channels),
            jnp.dot(inputs_t[0:channels, :], hid_buf[...], preferred_element_type=F32),
        )
        put(
            slice(channels, time_end),
            jnp.dot(inputs_t[channels:, :], pre_buf[...], preferred_element_type=F32),
        )
        grad_out = jnp.dot(grad_t, hid[...], preferred_element_type=F32)
        put(
            slice(time_end, out.shape[0]),
            grad_out * factor[0:1, :] + grad_sum * shift[0:1, :],
        )

    return backward_kernel


def backward(stats, target_t, state, weights, factor, shift, inputs_t, before, sizes):
    rows, columns = state[0].shape
    scratch = [
        pltpu.VMEM((rows, columns), F32),
        pltpu.VMEM((rows, columns), BF16),
        pltpu.VMEM((rows, columns), BF16),
        pltpu.VMEM((rows, LANES), F32),
    ]
    flops = 2 * rows * columns * (weights.shape[0] + target_t.shape[0])
    args = (*stats, target_t, *state, weights, factor, shift, inputs_t, *before)
    outs = [(weights.shape, BF16 if before else F32)]
    kernel = make_backward_kernel(*sizes, bool(before))
    return local_call(kernel, "backward", args, outs, scratch, flops=flops)[0]


def prepare_kernel(
    core, latents, latents_got, noise, noise_got, levels, levels_got, modulation, *rest
):
    outs, (latent_buf, noise_buf, level_buf) = rest[:-3], rest[-3:]
    steps, channels, tokens = latents.shape
    half_width = (outs[0].shape[0] - channels) // 2
    pairs = ((latents, latents_got), (noise, noise_got), (levels, levels_got))
    for buffer, (own, got) in zip((latent_buf, noise_buf, level_buf), pairs):

        @pl.when(core[0] == 0)
        def _():
            buffer[0] = own[...]
            buffer[1] = got[...]

        @pl.when(core[0] != 0)
        def _():
            buffer[0] = got[...]
            buffer[1] = own[...]

    place = 0
    for step in range(steps):
        for owner in range(CORES):
            inputs_t, target_t = outs[place : place + 2]
            place += 2
            level = (level_buf[owner, step : step + 1, :].astype(F32) + 0.5) / LEVELS
            latent = latent_buf[owner, step].astype(F32)
            draw = noise_buf[owner, step].astype(F32)
            noised = ((1.0 - level) * latent + level * draw).astype(BF16).astype(F32)
            noised = noised * (1.0 / math.sqrt(channels))
            inputs_t[0:channels, :] = noised.astype(BF16)
            target_t[...] = draw - latent
            order = lax.broadcasted_iota(jnp.int32, (half_width, tokens), 0).astype(F32)
            angles = (1000.0 * level) * jnp.exp(-math.log(10000.0) * order / half_width)
            root = 0.5 / math.sqrt(2 * half_width)
            for part, wave in enumerate((jnp.cos(angles), jnp.sin(angles))):
                wave = wave.astype(BF16).astype(F32) * root
                inputs_t[pl.ds(channels + part * half_width, half_width), :] = wave.astype(BF16)
    rows = modulation[...]
    half = rows.shape[1] // CORES
    factor, shift, terms = outs[place:]

    for side in range(CORES):

        @pl.when(core[0] == side)
        def _():
            here = rows[:, side * half : (side + 1) * half]
            factor[...] = 1.0 + here[1:2]
            shift[...] = here[0:1]
            wide = jnp.broadcast_to(here[0:1], terms.shape)
            high = wide.astype(BF16).astype(F32)
            index = lax.broadcasted_iota(jnp.int32, terms.shape, 0)
            split = jnp.where(index == 0, high, jnp.where(index == 1, wide - high, 0.0))
            terms[...] = split.astype(BF16)


def prepare(core, latents, noise_draw, timesteps, mod_rows, time_width, width):
    steps, tokens, channels = latents.shape
    half = mod_rows.shape[1] // CORES
    outs = [
        ((channels + time_width, tokens), BF16),
        ((channels, tokens), F32),
    ] * (steps * CORES) + [((1, half), F32), ((1, half), F32), ((16, half), BF16)]
    args = []
    scratch = []
    for values in (latents.transpose(0, 2, 1), noise_draw.transpose(0, 2, 1), timesteps):
        args += [values, core_swap(values, width)]
        scratch.append(pltpu.VMEM((CORES,) + values.shape, values.dtype))
    results = local_call(
        prepare_kernel,
        "prepare",
        (*args, mod_rows),
        outs,
        scratch,
        scalars=(core,),
        flops=2**32,
    )
    sets = [results[2 * i : 2 * i + 2] for i in range(steps * CORES)]
    return [sets[CORES * s : CORES * (s + 1)] for s in range(steps)], results[-3:]


def step_kernel(blocks, params, mean, square, new_mean, new_square, new_params, copies):
    first, second, new = adam(blocks, params, mean, square)
    new_mean[...] = first
    new_square[...] = second
    new_params[...] = new
    block = new.astype(BF16)
    for chip in range(copies.shape[0]):
        copies[chip] = block


def last_kernel(blocks, params, mean, square, start, new_mean, new_square, strips):
    first, second, new = adam(blocks, params, mean, square)
    new_mean[...] = first
    new_square[...] = second
    drift = (start[...] - new).astype(BF16)
    rows, columns = strips.shape[1:]
    used = 0
    for top in range(0, drift.shape[0], rows):
        for left in range(0, drift.shape[1], columns):
            strips[used] = drift[top : top + rows, left : left + columns]
            used += 1
    for index in range(used, strips.shape[0]):
        strips[index] = jnp.zeros((rows, columns), BF16)


def adam(blocks, params, mean, square):
    gradient = blocks[0].astype(F32)
    for chip in range(1, blocks.shape[0]):
        gradient = gradient + blocks[chip].astype(F32)
    old = params[...]
    first = BETA_ONE * mean[...] + (1.0 - BETA_ONE) * gradient
    second = BETA_TWO * square[...] + (1.0 - BETA_TWO) * gradient * gradient
    new = old - INNER_RATE * (first / (jnp.sqrt(second) + ADAM_EPS) + DECAY_RATE * old)
    return first, second, new


def strip_sum_kernel(strips, copies):
    total = strips[0].astype(F32)
    for index in range(1, strips.shape[0]):
        total = total + strips[index].astype(F32)
    block = total.astype(BF16)
    for index in range(copies.shape[0]):
        copies[index] = block


def make_outer_kernel(replicas):
    def outer_kernel(core, own, got, params, momentum, new_params, new_momentum, own_buf, got_buf):
        strip_rows, strip_columns = own.shape[1:]
        rows = params.shape[0]
        half = params.shape[1] // CORES
        index = 0
        for top in range(0, rows * CORES, strip_rows):
            for left in range(0, half, strip_columns):
                place = (slice(top, top + strip_rows), slice(left, left + strip_columns))
                own_buf[place] = own[index].astype(F32)
                got_buf[place] = got[index].astype(F32)
                index += 1

        def finish(cols, values):
            average = values * (1.0 / replicas)
            moved = NESTEROV * momentum[:, cols] + average
            new_momentum[:, cols] = moved
            new_params[:, cols] = params[:, cols] - OUTER_RATE * (average + NESTEROV * moved)

        @pl.when(core[0] == 0)
        def _():
            finish(slice(0, half), own_buf[0:rows])
            finish(slice(half, 2 * half), got_buf[0:rows])

        @pl.when(core[0] != 0)
        def _():
            finish(slice(0, half), got_buf[rows:])
            finish(slice(half, 2 * half), own_buf[rows:])

    return outer_kernel


def on_device(
    outer_params,
    outer_momentum,
    inner_mean,
    inner_square,
    latents,
    noise_draw,
    timesteps,
    fragment,
    modulation,
):
    width = lax.axis_size("fsdp")
    replicas = lax.axis_size("replica")
    chips = width // CORES
    core = (lax.axis_index("fsdp") % CORES).astype(jnp.int32)
    core_arg = core.reshape(1)
    rows, model_width = outer_params.shape
    half = model_width // CORES
    channels = latents.shape[2]
    time_width = rows * width - 2 * channels
    total_rows = latents.shape[1] * width

    pair_shape = (rows * CORES, half)
    start, copies = local_call(
        start_kernel,
        "start",
        (hold(outer_params), core_swap(outer_params, width)),
        [(pair_shape, F32), ((chips,) + pair_shape, BF16)],
        scalars=(core_arg,),
    )
    gathered = chip_exchange(copies, width)

    mod_rows = lax.dynamic_index_in_dim(modulation, fragment[0], 0, keepdims=False)
    prepared, mods = prepare(
        core_arg, latents, noise_draw, timesteps, mod_rows, time_width, width
    )
    params = start
    mean, square = local_call(
        moments_kernel,
        "moments",
        (
            inner_mean[0],
            core_swap(inner_mean[0], width),
            inner_square[0],
            core_swap(inner_square[0], width),
        ),
        [(pair_shape, F32)] * 2,
        scalars=(core_arg,),
    )
    gathered, prepared, mods, mean, square = lax.optimization_barrier(
        (gathered, prepared, mods, mean, square)
    )

    sizes = (model_width, total_rows)
    factor, shift, terms = mods
    for step in range(STEPS):
        weights = gathered.reshape(chips * pair_shape[0], half)
        states = []
        for inputs_t, _ in prepared[step]:
            hid, slope, stats = forward(inputs_t, weights, factor, terms)
            states.append(((hid, slope), (stats, core_swap(stats, width))))
        gradient = ()
        for (state, stats), (inputs_t, target_t) in zip(states, prepared[step]):
            gradient = (
                backward(
                    stats, target_t, state, weights, factor, shift, inputs_t, gradient, sizes
                ),
            )
        pair_sum = gradient[0]
        blocks = chip_exchange(pair_sum.reshape((chips,) + pair_shape), width)
        moments = [(pair_shape, F32)] * 2
        if step + 1 < STEPS:
            outs = moments + [(pair_shape, F32), ((chips,) + pair_shape, BF16)]
            mean, square, params, copies = local_call(
                step_kernel, "update", (blocks, params, mean, square), outs
            )
            gathered = chip_exchange(copies, width)
        else:
            strip = (STRIP_ROWS, half // STRIP_PARTS)
            outs = moments + [((replicas,) + strip, BF16)]
            mean, square, strips = local_call(
                last_kernel, "update_last", (blocks, params, mean, square, start), outs
            )
    strips = lax.all_to_all(strips, "replica", 0, 0)
    new_mean, new_square = local_call(
        unpair_kernel,
        "unpair",
        (mean, core_swap(mean, width), square, core_swap(square, width)),
        [(outer_params.shape, F32)] * 2,
        scalars=(core_arg,),
        hbm_outs=True,
    )
    strips, new_mean, new_square = lax.optimization_barrier((strips, new_mean, new_square))
    strips = local_call(strip_sum_kernel, "strip_sum", (strips,), [(strips.shape, BF16)])[0]
    strips = lax.all_to_all(strips, "replica", 0, 0)
    new_params, new_momentum = local_call(
        make_outer_kernel(replicas),
        "outer",
        (strips, core_swap(strips, width), outer_params, outer_momentum),
        [(outer_params.shape, F32)] * 2,
        [pltpu.VMEM(pair_shape, F32)] * 2,
        scalars=(core_arg,),
        hbm_outs=True,
    )
    return (new_params, new_momentum, new_mean[None], new_square[None])


def solution(mesh):
    return jax.shard_map(
        on_device,
        mesh=mesh,
        in_specs=(
            P("fsdp", None),
            P("fsdp", None),
            P("replica", "fsdp", None),
            P("replica", "fsdp", None),
            P(None, ("replica", "fsdp"), None),
            P(None, ("replica", "fsdp"), None),
            P(None, ("replica", "fsdp")),
            P(),
            P(),
        ),
        out_specs=(
            P("fsdp", None),
            P("fsdp", None),
            P("replica", "fsdp", None),
            P("replica", "fsdp", None),
        ),
        check_vma=False,
    )
```

```python
import math

import jax
import jax.numpy as jnp
from jax import lax
from jax.experimental import pallas as pl
from jax.experimental.pallas import tpu as pltpu
from jax.sharding import PartitionSpec as P

STEPS = 2
LEVELS = 1000


BETA_ONE = 0.9
BETA_TWO = 0.95
INNER_RATE = 0.2
DECAY_RATE = 0.1
ADAM_EPS = 1e-08
NORM_EPS = 1e-06
OUTER_RATE = 0.7
NESTEROV = 0.9

CORES = 2
LANES = 128
ROW_CHUNK = 16
FWD_COLUMNS = 256
STRIP_COLUMNS = 256
KERNEL_VMEM = 24 * 2**20

BF16 = jnp.bfloat16
F32 = jnp.float32
VMEM = pl.BlockSpec(memory_space=pltpu.VMEM)
SMEM = pl.BlockSpec(memory_space=pltpu.SMEM)
TRANSPOSED = (((1,), (1,)), ((), ()))
BOTH_TRANSPOSED = (((0,), (0,)), ((), ()))


def local_call(kernel, name, args, outs, scratch=(), scalars=(), flops=0, hbm_outs=False):
    place = pltpu.VMEM if not hbm_outs else jax.ShapeDtypeStruct
    specs = [SMEM] * len(scalars) + [VMEM] * len(args)
    values = [*scalars, *(pltpu.with_memory_space_constraint(a, pltpu.VMEM) for a in args)]
    moved = sum(math.prod(o[0]) * 4 for o in outs) + sum(a.size * a.dtype.itemsize for a in args)
    return pl.pallas_call(
        kernel,
        in_specs=specs,
        out_specs=[VMEM] * len(outs),
        out_shape=[place(shape, dtype) for shape, dtype in outs],
        scratch_shapes=list(scratch),
        compiler_params=pltpu.CompilerParams(vmem_limit_bytes=KERNEL_VMEM),
        cost_estimate=pl.CostEstimate(flops=flops, bytes_accessed=moved, transcendentals=0),
        name=name,
    )(*values)


def core_swap(values, width):
    return lax.ppermute(values, "fsdp", [(i, i ^ 1) for i in range(width)])


def exchange(blocks, axis):
    return lax.all_to_all(blocks, axis, 0, 0)


def spread_halves(values, copies):
    half = values.shape[1] // CORES
    for core in range(CORES):
        block = values[:, core * half : (core + 1) * half].astype(BF16)
        for index in range(core, copies.shape[0], CORES):
            copies[index] = block


def start_kernel(params, copies):
    spread_halves(params[...], copies)


def scaled_out_weight(weights, factor, time_end):
    return (weights[time_end:, :].astype(F32) * factor[0:1, :]).astype(BF16)


def forward_kernel(inputs_t, weights, factor, shift, hid, slope, stats, pre_buf, in_buf, square):
    time_end, rows_here = inputs_t.shape
    channels = weights.shape[0] - time_end
    square[...] = jnp.zeros_like(square)
    for index in range(weights.shape[1] // FWD_COLUMNS):
        slot = index % 2
        cols = pl.ds(index * FWD_COLUMNS, FWD_COLUMNS)
        pre_buf[slot] = lax.dot_general(
            inputs_t[channels:, :],
            weights[channels:time_end, cols],
            BOTH_TRANSPOSED,
            preferred_element_type=F32,
        )
        in_buf[slot] = lax.dot_general(
            inputs_t[0:channels, :],
            weights[0:channels, cols],
            BOTH_TRANSPOSED,
            preferred_element_type=F32,
        )
        for start in range(0, rows_here, ROW_CHUNK):
            rows = pl.ds(start, ROW_CHUNK)
            half_pre = pre_buf[slot, rows, :]
            wave = jnp.tanh(half_pre)
            above = wave + 1.0
            silu = half_pre * above
            hidden = in_buf[slot, rows, :] + silu
            hid[rows, cols] = hidden.astype(BF16)
            slope[rows, cols] = (above + silu * (1.0 - wave)).astype(BF16)
            power = hidden * hidden
            partial = power[:, 0:LANES]
            for lane in range(LANES, FWD_COLUMNS, LANES):
                partial = partial + power[:, lane : lane + LANES]
            square[rows, :] += partial
    scaled = scaled_out_weight(weights, factor, time_end)
    out = lax.dot_general(hid[...], scaled, TRANSPOSED, preferred_element_type=F32)
    bias = lax.dot_general(
        shift[...], weights[time_end:, :], TRANSPOSED, preferred_element_type=F32
    )
    power = jnp.sum(square[...], axis=1, keepdims=True)
    stats[0:rows_here, :] = jnp.concatenate(
        [out, jnp.broadcast_to(power, (rows_here, LANES - channels))], axis=1
    )
    stats[rows_here:, :] = jnp.concatenate([bias, jnp.zeros_like(bias)], axis=1)


def forward(inputs_t, weights, factor, shift):
    rows, columns = inputs_t.shape[1], weights.shape[1]
    outs = [((rows, columns), BF16)] * 2 + [((rows + shift.shape[0], LANES), F32)]
    scratch = [pltpu.VMEM((2, rows, FWD_COLUMNS), F32)] * 2 + [pltpu.VMEM((rows, LANES), F32)]
    flops = 2 * rows * columns * weights.shape[0]
    args = (inputs_t, weights, factor, shift)
    return local_call(forward_kernel, "forward", args, outs, scratch, flops=flops)


def make_backward_kernel(model_width, total_rows, added):
    def backward_kernel(
        own, got, target_t, hid, slope, weights, factor, shift, inputs_t, *rest
    ):
        before = rest[0] if added else None
        out, mod_buf, hid_buf, pre_buf, pull = rest[1:] if added else rest
        root = 1.0 / math.sqrt(model_width)
        channels, rows_here = target_t.shape
        time_end = inputs_t.shape[0]
        columns = out.shape[1]

        both = own[0:rows_here, :] + got[0:rows_here, :]
        raw = both[:, 0:channels]
        inverse = lax.rsqrt(both[:, channels : channels + 1] * (1.0 / model_width) + NORM_EPS)
        terms = own[rows_here:, 0:channels] + got[rows_here:, 0:channels]
        bias = jnp.sum(terms, axis=0, keepdims=True)
        output = (inverse * raw + bias) * root
        out_grad = (2.0 / (total_rows * channels)) * (output - target_t[...].T)
        grad = (out_grad * (inverse * root)).astype(BF16)
        wide = grad.astype(F32)
        grad_t = wide.T.astype(BF16)
        pulled = inverse * inverse * (1.0 / model_width)
        pulled = pulled * jnp.sum(wide * raw, axis=1, keepdims=True)
        pull[...] = jnp.broadcast_to(pulled, pull.shape)
        grad_sum = jnp.sum(out_grad.T, axis=1, keepdims=True) * root

        scaled = scaled_out_weight(weights, factor, time_end)
        mod_buf[...] = jnp.dot(grad, scaled, preferred_element_type=F32)
        for start in range(0, rows_here, ROW_CHUNK):
            rows = pl.ds(start, ROW_CHUNK)
            spread = jnp.concatenate([pull[rows, :]] * (columns // LANES), axis=1)
            hid_grad = mod_buf[rows, :] - hid[rows, :].astype(F32) * spread
            hid_buf[rows, :] = hid_grad.astype(BF16)
            pre_buf[rows, :] = (hid_grad * slope[rows, :].astype(F32)).astype(BF16)

        def put(rows, values):
            if added:
                values = values + before[rows, :]
            out[rows, :] = values.astype(out.dtype)

        put(
            slice(0, channels),
            jnp.dot(inputs_t[0:channels, :], hid_buf[...], preferred_element_type=F32),
        )
        put(
            slice(channels, time_end),
            jnp.dot(inputs_t[channels:, :], pre_buf[...], preferred_element_type=F32),
        )
        grad_out = jnp.dot(grad_t, hid[...], preferred_element_type=F32)
        put(
            slice(time_end, out.shape[0]),
            grad_out * factor[0:1, :] + grad_sum * shift[0:1, :],
        )

    return backward_kernel


def backward(stats, target_t, state, weights, factor, shift, inputs_t, before, sizes):
    rows, columns = state[0].shape
    scratch = [
        pltpu.VMEM((rows, columns), F32),
        pltpu.VMEM((rows, columns), BF16),
        pltpu.VMEM((rows, columns), BF16),
        pltpu.VMEM((rows, LANES), F32),
    ]
    flops = 2 * rows * columns * (weights.shape[0] + target_t.shape[0])
    args = (*stats, target_t, *state, weights, factor, shift, inputs_t, *before)
    outs = [(weights.shape, BF16 if before else F32)]
    kernel = make_backward_kernel(*sizes, bool(before))
    return local_call(kernel, "backward", args, outs, scratch, flops=flops)[0]


def prepare_kernel(
    core, latents, latents_got, noise, noise_got, levels, levels_got, modulation, *rest
):
    outs, (latent_buf, noise_buf, level_buf) = rest[:-3], rest[-3:]
    steps, channels, tokens = latents.shape
    half_width = (outs[0].shape[0] - channels) // 2
    pairs = ((latents, latents_got), (noise, noise_got), (levels, levels_got))
    for buffer, (own, got) in zip((latent_buf, noise_buf, level_buf), pairs):

        @pl.when(core[0] == 0)
        def _():
            buffer[0] = own[...]
            buffer[1] = got[...]

        @pl.when(core[0] != 0)
        def _():
            buffer[0] = got[...]
            buffer[1] = own[...]

    place = 0
    for step in range(steps):
        for owner in range(CORES):
            inputs_t, target_t = outs[place : place + 2]
            place += 2
            level = (level_buf[owner, step : step + 1, :].astype(F32) + 0.5) / LEVELS
            latent = latent_buf[owner, step].astype(F32)
            draw = noise_buf[owner, step].astype(F32)
            noised = ((1.0 - level) * latent + level * draw).astype(BF16).astype(F32)
            noised = noised * (1.0 / math.sqrt(channels))
            inputs_t[0:channels, :] = noised.astype(BF16)
            target_t[...] = draw - latent
            order = lax.broadcasted_iota(jnp.int32, (half_width, tokens), 0).astype(F32)
            angles = (1000.0 * level) * jnp.exp(-math.log(10000.0) * order / half_width)
            root = 0.5 / math.sqrt(2 * half_width)
            for part, wave in enumerate((jnp.cos(angles), jnp.sin(angles))):
                wave = wave.astype(BF16).astype(F32) * root
                inputs_t[pl.ds(channels + part * half_width, half_width), :] = wave.astype(BF16)
    rows = modulation[...]
    half = rows.shape[1] // CORES
    factor, shift, terms = outs[place:]

    for side in range(CORES):

        @pl.when(core[0] == side)
        def _():
            here = rows[:, side * half : (side + 1) * half]
            factor[...] = 1.0 + here[1:2]
            shift[...] = here[0:1]
            wide = jnp.broadcast_to(here[0:1], terms.shape)
            high = wide.astype(BF16).astype(F32)
            index = lax.broadcasted_iota(jnp.int32, terms.shape, 0)
            split = jnp.where(index == 0, high, jnp.where(index == 1, wide - high, 0.0))
            terms[...] = split.astype(BF16)


def prepare(core, latents, noise_draw, timesteps, mod_rows, time_width, width):
    steps, tokens, channels = latents.shape
    half = mod_rows.shape[1] // CORES
    outs = [
        ((channels + time_width, tokens), BF16),
        ((channels, tokens), F32),
    ] * (steps * CORES) + [((1, half), F32), ((1, half), F32), ((16, half), BF16)]
    args = []
    scratch = []
    for values in (latents.transpose(0, 2, 1), noise_draw.transpose(0, 2, 1), timesteps):
        args += [values, core_swap(values, width)]
        scratch.append(pltpu.VMEM((CORES,) + values.shape, values.dtype))
    results = local_call(
        prepare_kernel,
        "prepare",
        (*args, mod_rows),
        outs,
        scratch,
        scalars=(core,),
        flops=2**32,
    )
    sets = [results[2 * i : 2 * i + 2] for i in range(steps * CORES)]
    return [sets[CORES * s : CORES * (s + 1)] for s in range(steps)], results[-3:]


def adam(blocks, params, mean, square):
    halves = []
    for core in range(CORES):
        total = blocks[core].astype(F32)
        for index in range(core + CORES, blocks.shape[0], CORES):
            total = total + blocks[index].astype(F32)
        halves.append(total)
    gradient = jnp.concatenate(halves, axis=1)
    old = params[...]
    first = BETA_ONE * mean[...] + (1.0 - BETA_ONE) * gradient
    second = BETA_TWO * square[...] + (1.0 - BETA_TWO) * gradient * gradient
    new = old - INNER_RATE * (first / (jnp.sqrt(second) + ADAM_EPS) + DECAY_RATE * old)
    return first, second, new


def step_kernel(blocks, params, mean, square, new_mean, new_square, new_params, copies):
    first, second, new = adam(blocks, params, mean, square)
    new_mean[...] = first
    new_square[...] = second
    new_params[...] = new
    spread_halves(new, copies)


def last_kernel(blocks, params, mean, square, start, new_mean, new_square, strips):
    first, second, new = adam(blocks, params, mean, square)
    new_mean[...] = first
    new_square[...] = second
    drift = start[...] - new
    width = strips.shape[2]
    for index in range(strips.shape[0]):
        if index * width < drift.shape[1]:
            strips[index] = drift[:, index * width : (index + 1) * width].astype(BF16)
        else:
            strips[index] = jnp.zeros(strips.shape[1:], BF16)


def strip_sum_kernel(strips, copies):
    total = strips[0].astype(F32)
    for index in range(1, strips.shape[0]):
        total = total + strips[index].astype(F32)
    block = total.astype(BF16)
    for index in range(copies.shape[0]):
        copies[index] = block


def make_outer_kernel(replicas):
    def outer_kernel(strips, params, momentum, new_params, new_momentum):
        width = strips.shape[2]
        for index in range(params.shape[1] // width):
            cols = slice(index * width, (index + 1) * width)
            average = strips[index].astype(F32) * (1.0 / replicas)
            moved = NESTEROV * momentum[:, cols] + average
            new_momentum[:, cols] = moved
            new_params[:, cols] = params[:, cols] - OUTER_RATE * (average + NESTEROV * moved)

    return outer_kernel


def on_device(
    outer_params,
    outer_momentum,
    inner_mean,
    inner_square,
    latents,
    noise_draw,
    timesteps,
    fragment,
    modulation,
):
    width = lax.axis_size("fsdp")
    replicas = lax.axis_size("replica")
    core = (lax.axis_index("fsdp") % CORES).astype(jnp.int32).reshape(1)
    rows, model_width = outer_params.shape
    half = model_width // CORES
    channels = latents.shape[2]
    time_width = rows * width - 2 * channels
    total_rows = latents.shape[1] * width
    blocks_shape = (width, rows, half)

    copies = local_call(start_kernel, "start", (outer_params,), [(blocks_shape, BF16)])[0]
    gathered = exchange(copies, "fsdp")
    mod_rows = lax.dynamic_index_in_dim(modulation, fragment[0], 0, keepdims=False)
    prepared, mods = prepare(
        core, latents, noise_draw, timesteps, mod_rows, time_width, width
    )
    gathered, prepared, mods = lax.optimization_barrier((gathered, prepared, mods))

    params, mean, square = outer_params, inner_mean[0], inner_square[0]
    sizes = (model_width, total_rows)
    factor, shift, terms = mods
    moments = [(params.shape, F32)] * 2
    for step in range(STEPS):
        weights = gathered.reshape(width * rows, half)
        states = []
        for inputs_t, _ in prepared[step]:
            hid, slope, stats = forward(inputs_t, weights, factor, terms)
            states.append(((hid, slope), (stats, core_swap(stats, width))))
        gradient = ()
        for (state, stats), (inputs_t, target_t) in zip(states, prepared[step]):
            gradient = (
                backward(
                    stats, target_t, state, weights, factor, shift, inputs_t, gradient, sizes
                ),
            )
        blocks = exchange(gradient[0].reshape(blocks_shape), "fsdp")
        if step + 1 < STEPS:
            mean, square, params, copies = local_call(
                step_kernel,
                "update",
                (blocks, params, mean, square),
                moments + [(params.shape, F32), (blocks_shape, BF16)],
            )
            gathered = exchange(copies, "fsdp")
        else:
            strips_shape = (replicas, rows, STRIP_COLUMNS)
            mean, square, strips = local_call(
                last_kernel,
                "update_last",
                (blocks, params, mean, square, outer_params),
                moments + [(strips_shape, BF16)],
            )
    strips = exchange(strips, "replica")
    strips = local_call(strip_sum_kernel, "strip_sum", (strips,), [(strips_shape, BF16)])[0]
    strips = exchange(strips, "replica")
    new_params, new_momentum = local_call(
        make_outer_kernel(replicas),
        "outer",
        (strips, outer_params, outer_momentum),
        [(params.shape, F32)] * 2,
        hbm_outs=True,
    )
    return (new_params, new_momentum, mean[None], square[None])


def solution(mesh):
    return jax.shard_map(
        on_device,
        mesh=mesh,
        in_specs=(
            P("fsdp", None),
            P("fsdp", None),
            P("replica", "fsdp", None),
            P("replica", "fsdp", None),
            P(None, ("replica", "fsdp"), None),
            P(None, ("replica", "fsdp"), None),
            P(None, ("replica", "fsdp")),
            P(),
            P(),
        ),
        out_specs=(
            P("fsdp", None),
            P("fsdp", None),
            P("replica", "fsdp", None),
            P("replica", "fsdp", None),
        ),
        check_vma=False,
    )
```

```python
import math

import jax
import jax.numpy as jnp
from jax import lax
from jax.experimental import pallas as pl
from jax.experimental.pallas import tpu as pltpu
from jax.sharding import PartitionSpec as P

STEPS = 2
LEVELS = 1000


BETA_ONE = 0.9
BETA_TWO = 0.95
INNER_RATE = 0.2
DECAY_RATE = 0.1
ADAM_EPS = 1e-08
NORM_EPS = 1e-06
OUTER_RATE = 0.7
NESTEROV = 0.9

CORES = 2
LANES = 128
ROW_CHUNK = 16
FWD_COLUMNS = 256
STRIP_COLUMNS = 256
KERNEL_VMEM = 24 * 2**20

BF16 = jnp.bfloat16
F32 = jnp.float32
VMEM = pl.BlockSpec(memory_space=pltpu.VMEM)
SMEM = pl.BlockSpec(memory_space=pltpu.SMEM)
RIGHT_TRANSPOSED = (((1,), (1,)), ((), ()))
LEFT_TRANSPOSED = (((0,), (0,)), ((), ()))
SHIFT_ROWS = 16


def local_call(kernel, name, args, outs, scratch=(), scalars=(), flops=0, hbm_outs=False):
    place = pltpu.VMEM if not hbm_outs else jax.ShapeDtypeStruct
    specs = [SMEM] * len(scalars) + [VMEM] * len(args)
    values = [*scalars, *(pltpu.with_memory_space_constraint(a, pltpu.VMEM) for a in args)]
    moved = sum(math.prod(o[0]) * 4 for o in outs) + sum(a.size * a.dtype.itemsize for a in args)
    return pl.pallas_call(
        kernel,
        in_specs=specs,
        out_specs=[VMEM] * len(outs),
        out_shape=[place(shape, dtype) for shape, dtype in outs],
        scratch_shapes=list(scratch),
        compiler_params=pltpu.CompilerParams(vmem_limit_bytes=KERNEL_VMEM),
        cost_estimate=pl.CostEstimate(flops=flops, bytes_accessed=moved, transcendentals=0),
        name=name,
    )(*values)


def core_swap(values, width):
    return lax.ppermute(values, "fsdp", [(i, i ^ 1) for i in range(width)])


def exchange(blocks, axis):
    return lax.all_to_all(blocks, axis, 0, 0)


def spread_halves(values, copies):
    half = values.shape[1] // CORES
    for core in range(CORES):
        block = values[:, core * half : (core + 1) * half].astype(BF16)
        for index in range(core, copies.shape[0], CORES):
            copies[index] = block


def start_kernel(params, copies):
    block = params[...].astype(BF16)
    for index in range(copies.shape[0]):
        copies[index, 0] = block


def spread_start(params, width):
    rows, columns = params.shape
    half = columns // CORES
    shape = (width // CORES, CORES, rows, half)
    copies = pl.pallas_call(
        start_kernel,
        grid=(CORES,),
        in_specs=[pl.BlockSpec((rows, half), lambda core: (0, core))],
        out_specs=pl.BlockSpec((shape[0], 1, rows, half), lambda core: (0, core, 0, 0)),
        out_shape=jax.ShapeDtypeStruct(shape, BF16),
        compiler_params=pltpu.CompilerParams(vmem_limit_bytes=KERNEL_VMEM),
        name="start",
    )(pltpu.with_memory_space_constraint(params, pltpu.HBM))
    return copies.reshape(width, rows, half)


def forward_kernel(inputs_t, weights, factor, shift, hid, slope, stats, pre_buf, in_buf, square):
    time_end, rows_here = inputs_t.shape
    channels = weights.shape[0] - time_end
    square[...] = jnp.zeros_like(square)
    for index in range(weights.shape[1] // FWD_COLUMNS):
        slot = index % 2
        cols = pl.ds(index * FWD_COLUMNS, FWD_COLUMNS)
        pre_buf[slot] = lax.dot_general(
            inputs_t[channels:, :],
            weights[channels:time_end, cols],
            LEFT_TRANSPOSED,
            preferred_element_type=F32,
        )
        in_buf[slot] = lax.dot_general(
            inputs_t[0:channels, :],
            weights[0:channels, cols],
            LEFT_TRANSPOSED,
            preferred_element_type=F32,
        )
        for start in range(0, rows_here, ROW_CHUNK):
            rows = pl.ds(start, ROW_CHUNK)
            half_pre = pre_buf[slot, rows, :]
            wave = jnp.tanh(half_pre)
            above = wave + 1.0
            silu = half_pre * above
            hidden = in_buf[slot, rows, :] + silu
            hid[rows, cols] = hidden.astype(BF16)
            slope[rows, cols] = (above + silu * (1.0 - wave)).astype(BF16)
            power = hidden * hidden
            partial = power[:, 0:LANES]
            for lane in range(LANES, FWD_COLUMNS, LANES):
                partial = partial + power[:, lane : lane + LANES]
            square[rows, :] += partial
    out_weight = weights[time_end:, :]
    scaled = (out_weight.astype(F32) * factor[0:1, :]).astype(BF16)
    out = lax.dot_general(hid[...], scaled, RIGHT_TRANSPOSED, preferred_element_type=F32)
    wide = jnp.broadcast_to(shift[0:1, :], (SHIFT_ROWS, shift.shape[1]))
    high = wide.astype(BF16).astype(F32)
    row = lax.broadcasted_iota(jnp.int32, wide.shape, 0)
    terms = jnp.where(row == 0, high, jnp.where(row == 1, wide - high, 0.0)).astype(BF16)
    bias = lax.dot_general(terms, out_weight, RIGHT_TRANSPOSED, preferred_element_type=F32)
    power = jnp.sum(square[...], axis=1, keepdims=True)
    stats[0:rows_here, :] = jnp.concatenate(
        [out, jnp.broadcast_to(power, (rows_here, LANES - channels))], axis=1
    )
    stats[rows_here:, :] = jnp.concatenate([bias, jnp.zeros_like(bias)], axis=1)


def forward(inputs_t, weights, factor, shift):
    rows, columns = inputs_t.shape[1], weights.shape[1]
    outs = [((rows, columns), BF16)] * 2 + [((rows + SHIFT_ROWS, LANES), F32)]
    scratch = [pltpu.VMEM((2, rows, FWD_COLUMNS), F32)] * 2 + [pltpu.VMEM((rows, LANES), F32)]
    flops = 2 * rows * columns * weights.shape[0]
    args = (inputs_t, weights, factor, shift)
    return local_call(forward_kernel, "forward", args, outs, scratch, flops=flops)


def make_backward_kernel(model_width, total_rows, added):
    def backward_kernel(
        own, got, target_t, hid, slope, weights, factor, shift, inputs_t, *rest
    ):
        before = rest[0] if added else None
        out, mod_buf, hid_buf, pre_buf, pull = rest[1:] if added else rest
        root = 1.0 / math.sqrt(model_width)
        channels, rows_here = target_t.shape
        time_end = inputs_t.shape[0]
        columns = out.shape[1]

        both = own[0:rows_here, :] + got[0:rows_here, :]
        raw = both[:, 0:channels]
        inverse = lax.rsqrt(both[:, channels : channels + 1] * (1.0 / model_width) + NORM_EPS)
        terms = own[rows_here:, 0:channels] + got[rows_here:, 0:channels]
        bias = jnp.sum(terms, axis=0, keepdims=True)
        output = (inverse * raw + bias) * root
        out_grad = (2.0 / (total_rows * channels)) * (output - target_t[...].T)
        grad = (out_grad * (inverse * root)).astype(BF16)
        wide = grad.astype(F32)
        grad_t = wide.T.astype(BF16)
        pulled = inverse * inverse * (1.0 / model_width)
        pulled = pulled * jnp.sum(wide * raw, axis=1, keepdims=True)
        pull[...] = jnp.broadcast_to(pulled, pull.shape)
        grad_sum = jnp.sum(out_grad.T, axis=1, keepdims=True) * root

        scaled = (weights[time_end:, :].astype(F32) * factor[0:1, :]).astype(BF16)
        mod_buf[...] = jnp.dot(grad, scaled, preferred_element_type=F32)
        for start in range(0, rows_here, ROW_CHUNK):
            rows = pl.ds(start, ROW_CHUNK)
            spread = jnp.concatenate([pull[rows, :]] * (columns // LANES), axis=1)
            hid_grad = mod_buf[rows, :] - hid[rows, :].astype(F32) * spread
            hid_buf[rows, :] = hid_grad.astype(BF16)
            pre_buf[rows, :] = (hid_grad * slope[rows, :].astype(F32)).astype(BF16)

        def put(rows, values):
            if added:
                values = values + before[rows, :]
            out[rows, :] = values.astype(out.dtype)

        put(
            slice(0, channels),
            jnp.dot(inputs_t[0:channels, :], hid_buf[...], preferred_element_type=F32),
        )
        put(
            slice(channels, time_end),
            jnp.dot(inputs_t[channels:, :], pre_buf[...], preferred_element_type=F32),
        )
        grad_out = jnp.dot(grad_t, hid[...], preferred_element_type=F32)
        put(
            slice(time_end, out.shape[0]),
            grad_out * factor[0:1, :] + grad_sum * shift[0:1, :],
        )

    return backward_kernel


def backward(stats, target_t, state, weights, factor, shift, inputs_t, before, sizes):
    rows, columns = state[0].shape
    scratch = [
        pltpu.VMEM((rows, columns), F32),
        pltpu.VMEM((rows, columns), BF16),
        pltpu.VMEM((rows, columns), BF16),
        pltpu.VMEM((rows, LANES), F32),
    ]
    flops = 2 * rows * columns * (weights.shape[0] + target_t.shape[0])
    args = (*stats, target_t, *state, weights, factor, shift, inputs_t, *before)
    outs = [(weights.shape, BF16 if before else F32)]
    kernel = make_backward_kernel(*sizes, bool(before))
    return local_call(kernel, "backward", args, outs, scratch, flops=flops)[0]


def prepare_kernel(
    core, latents, latents_got, noise, noise_got, levels, levels_got, modulation, *rest
):
    outs, (latent_buf, noise_buf, level_buf) = rest[:-3], rest[-3:]
    steps, channels, tokens = latents.shape
    half_width = (outs[0].shape[0] - channels) // 2
    pairs = ((latents, latents_got), (noise, noise_got), (levels, levels_got))
    for buffer, (own, got) in zip((latent_buf, noise_buf, level_buf), pairs):

        @pl.when(core[0] == 0)
        def _():
            buffer[0] = own[...]
            buffer[1] = got[...]

        @pl.when(core[0] != 0)
        def _():
            buffer[0] = got[...]
            buffer[1] = own[...]

    place = 0
    for step in range(steps):
        for owner in range(CORES):
            inputs_t, target_t = outs[place : place + 2]
            place += 2
            level = (level_buf[owner, step : step + 1, :].astype(F32) + 0.5) / LEVELS
            latent = latent_buf[owner, step].astype(F32)
            draw = noise_buf[owner, step].astype(F32)
            noised = ((1.0 - level) * latent + level * draw).astype(BF16).astype(F32)
            noised = noised * (1.0 / math.sqrt(channels))
            inputs_t[0:channels, :] = noised.astype(BF16)
            target_t[...] = draw - latent
            order = lax.broadcasted_iota(jnp.int32, (half_width, tokens), 0).astype(F32)
            angles = (1000.0 * level) * jnp.exp(-math.log(10000.0) * order / half_width)
            root = 0.5 / math.sqrt(2 * half_width)
            for part, wave in enumerate((jnp.cos(angles), jnp.sin(angles))):
                wave = wave.astype(BF16).astype(F32) * root
                inputs_t[pl.ds(channels + part * half_width, half_width), :] = wave.astype(BF16)
    rows = modulation[...]
    half = rows.shape[1] // CORES
    factor, shift = outs[place:]

    for side in range(CORES):

        @pl.when(core[0] == side)
        def _():
            here = rows[:, side * half : (side + 1) * half]
            factor[...] = 1.0 + here[1:2]
            shift[...] = here[0:1]


def prepare(core, latents, noise_draw, timesteps, mod_rows, time_width, width):
    steps, tokens, channels = latents.shape
    half = mod_rows.shape[1] // CORES
    outs = [
        ((channels + time_width, tokens), BF16),
        ((channels, tokens), F32),
    ] * (steps * CORES) + [((1, half), F32)] * 2
    args = []
    scratch = []
    for values in (latents.transpose(0, 2, 1), noise_draw.transpose(0, 2, 1), timesteps):
        args += [values, core_swap(values, width)]
        scratch.append(pltpu.VMEM((CORES,) + values.shape, values.dtype))
    results = local_call(
        prepare_kernel,
        "prepare",
        (*args, mod_rows),
        outs,
        scratch,
        scalars=(core,),
        flops=2**32,
    )
    sets = [results[2 * i : 2 * i + 2] for i in range(steps * CORES)]
    return [sets[CORES * s : CORES * (s + 1)] for s in range(steps)], results[-2:]


def adam(blocks, params, mean, square):
    halves = []
    for core in range(CORES):
        total = blocks[core].astype(F32)
        for index in range(core + CORES, blocks.shape[0], CORES):
            total = total + blocks[index].astype(F32)
        halves.append(total)
    gradient = jnp.concatenate(halves, axis=1)
    old = params[...]
    first = BETA_ONE * mean[...] + (1.0 - BETA_ONE) * gradient
    second = BETA_TWO * square[...] + (1.0 - BETA_TWO) * gradient * gradient
    new = old - INNER_RATE * (first / (jnp.sqrt(second) + ADAM_EPS) + DECAY_RATE * old)
    return first, second, new


def step_kernel(blocks, params, mean, square, new_mean, new_square, new_params, copies):
    first, second, new = adam(blocks, params, mean, square)
    new_mean[...] = first
    new_square[...] = second
    new_params[...] = new
    spread_halves(new, copies)


def last_kernel(blocks, params, mean, square, start, new_mean, new_square, strips):
    first, second, new = adam(blocks, params, mean, square)
    new_mean[...] = first
    new_square[...] = second
    drift = start[...] - new
    width = strips.shape[2]
    for index in range(strips.shape[0]):
        if index * width < drift.shape[1]:
            strips[index] = drift[:, index * width : (index + 1) * width].astype(BF16)
        else:
            strips[index] = jnp.zeros(strips.shape[1:], BF16)


def strip_sum_kernel(strips, copies):
    total = strips[0].astype(F32)
    for index in range(1, strips.shape[0]):
        total = total + strips[index].astype(F32)
    block = total.astype(BF16)
    for index in range(copies.shape[0]):
        copies[index] = block


def make_outer_kernel(replicas):
    def outer_kernel(strips, params, momentum, mean, square, new_params, new_momentum, *moments):
        moments[0][...] = mean[...]
        moments[1][...] = square[...]
        width = strips.shape[2]
        for index in range(params.shape[1] // width):
            cols = slice(index * width, (index + 1) * width)
            average = strips[index].astype(F32) * (1.0 / replicas)
            moved = NESTEROV * momentum[:, cols] + average
            new_momentum[:, cols] = moved
            new_params[:, cols] = params[:, cols] - OUTER_RATE * (average + NESTEROV * moved)

    return outer_kernel


def on_device(
    outer_params,
    outer_momentum,
    inner_mean,
    inner_square,
    latents,
    noise_draw,
    timesteps,
    fragment,
    modulation,
):
    width = lax.axis_size("fsdp")
    replicas = lax.axis_size("replica")
    core = (lax.axis_index("fsdp") % CORES).astype(jnp.int32).reshape(1)
    rows, model_width = outer_params.shape
    half = model_width // CORES
    channels = latents.shape[2]
    time_width = rows * width - 2 * channels
    total_rows = latents.shape[1] * width
    blocks_shape = (width, rows, half)

    gathered = exchange(spread_start(outer_params, width), "fsdp")
    mod_rows = lax.dynamic_index_in_dim(modulation, fragment[0], 0, keepdims=False)
    prepared, mods = prepare(
        core, latents, noise_draw, timesteps, mod_rows, time_width, width
    )
    gathered, prepared, mods = lax.optimization_barrier((gathered, prepared, mods))

    params, mean, square = outer_params, inner_mean[0], inner_square[0]
    sizes = (model_width, total_rows)
    factor, shift = mods
    moments = [(params.shape, F32)] * 2
    for step in range(STEPS):
        weights = gathered.reshape(width * rows, half)
        states = []
        for inputs_t, _ in prepared[step]:
            hid, slope, stats = forward(inputs_t, weights, factor, shift)
            states.append(((hid, slope), (stats, core_swap(stats, width))))
        gradient = ()
        for (state, stats), (inputs_t, target_t) in zip(states, prepared[step]):
            gradient = (
                backward(
                    stats, target_t, state, weights, factor, shift, inputs_t, gradient, sizes
                ),
            )
        blocks = exchange(gradient[0].reshape(blocks_shape), "fsdp")
        if step + 1 < STEPS:
            mean, square, params, copies = local_call(
                step_kernel,
                "update",
                (blocks, params, mean, square),
                moments + [(params.shape, F32), (blocks_shape, BF16)],
            )
            gathered = exchange(copies, "fsdp")
        else:
            strips_shape = (replicas, rows, STRIP_COLUMNS)
            mean, square, strips = local_call(
                last_kernel,
                "update_last",
                (blocks, params, mean, square, outer_params),
                moments + [(strips_shape, BF16)],
            )
    strips = exchange(strips, "replica")
    strips = local_call(strip_sum_kernel, "strip_sum", (strips,), [(strips_shape, BF16)])[0]
    strips = exchange(strips, "replica")
    new_params, new_momentum, mean, square = local_call(
        make_outer_kernel(replicas),
        "outer",
        (strips, outer_params, outer_momentum, mean, square),
        [(params.shape, F32)] * 4,
        hbm_outs=True,
    )
    return (new_params, new_momentum, mean[None], square[None])


def solution(mesh):
    return jax.shard_map(
        on_device,
        mesh=mesh,
        in_specs=(
            P("fsdp", None),
            P("fsdp", None),
            P("replica", "fsdp", None),
            P("replica", "fsdp", None),
            P(None, ("replica", "fsdp"), None),
            P(None, ("replica", "fsdp"), None),
            P(None, ("replica", "fsdp")),
            P(),
            P(),
        ),
        out_specs=(
            P("fsdp", None),
            P("fsdp", None),
            P("replica", "fsdp", None),
            P("replica", "fsdp", None),
        ),
        check_vma=False,
    )
```

```python
import math

import jax
import jax.numpy as jnp
from jax import lax
from jax.experimental import pallas as pl
from jax.experimental.pallas import tpu as pltpu
from jax.sharding import PartitionSpec as P

STEPS = 2
LEVELS = 1000


BETA_ONE = 0.9
BETA_TWO = 0.95
INNER_RATE = 0.2
DECAY_RATE = 0.1
ADAM_EPS = 1e-08
NORM_EPS = 1e-06
OUTER_RATE = 0.7
NESTEROV = 0.9

CORES = 2
LANES = 128
ROW_CHUNK = 16
FWD_COLUMNS = 256
KERNEL_VMEM = 24 * 2**20

BF16 = jnp.bfloat16
F32 = jnp.float32
VMEM = pl.BlockSpec(memory_space=pltpu.VMEM)
SMEM = pl.BlockSpec(memory_space=pltpu.SMEM)
RIGHT_TRANSPOSED = (((1,), (1,)), ((), ()))
LEFT_TRANSPOSED = (((0,), (0,)), ((), ()))
SHIFT_ROWS = 16


def local_call(kernel, name, args, outs, scratch=(), scalars=(), flops=0, hbm_outs=False):
    place = pltpu.VMEM if not hbm_outs else jax.ShapeDtypeStruct
    specs = [SMEM] * len(scalars) + [VMEM] * len(args)
    values = [*scalars, *(pltpu.with_memory_space_constraint(a, pltpu.VMEM) for a in args)]
    moved = sum(math.prod(o[0]) * 4 for o in outs) + sum(a.size * a.dtype.itemsize for a in args)
    return pl.pallas_call(
        kernel,
        in_specs=specs,
        out_specs=[VMEM] * len(outs),
        out_shape=[place(shape, dtype) for shape, dtype in outs],
        scratch_shapes=list(scratch),
        compiler_params=pltpu.CompilerParams(vmem_limit_bytes=KERNEL_VMEM),
        cost_estimate=pl.CostEstimate(flops=flops, bytes_accessed=moved, transcendentals=0),
        name=name,
    )(*values)


def core_swap(values, width):
    return lax.ppermute(values, "fsdp", [(i, i ^ 1) for i in range(width)])


def exchange(blocks, axis):
    return lax.all_to_all(blocks, axis, 0, 0)


def spread_halves(values, copies):
    half = values.shape[1] // CORES
    for core in range(CORES):
        block = values[:, core * half : (core + 1) * half].astype(BF16)
        for index in range(core, copies.shape[0], CORES):
            copies[index] = block


def start_kernel(params, copies):
    block = params[...].astype(BF16)
    for index in range(copies.shape[0]):
        copies[index, 0] = block


def spread_start(params, width):
    rows, columns = params.shape
    half = columns // CORES
    shape = (width // CORES, CORES, rows, half)
    copies = pl.pallas_call(
        start_kernel,
        grid=(CORES,),
        in_specs=[pl.BlockSpec((rows, half), lambda core: (0, core))],
        out_specs=pl.BlockSpec((shape[0], 1, rows, half), lambda core: (0, core, 0, 0)),
        out_shape=jax.ShapeDtypeStruct(shape, BF16),
        compiler_params=pltpu.CompilerParams(vmem_limit_bytes=KERNEL_VMEM),
        name="start",
    )(pltpu.with_memory_space_constraint(params, pltpu.HBM))
    return copies.reshape(width, rows, half)


def forward_kernel(inputs_t, weights, factor, shift, hid, slope, stats, pre_buf, in_buf, square):
    time_end, rows_here = inputs_t.shape
    channels = weights.shape[0] - time_end
    square[...] = jnp.zeros_like(square)
    for index in range(weights.shape[1] // FWD_COLUMNS):
        slot = index % 2
        cols = pl.ds(index * FWD_COLUMNS, FWD_COLUMNS)
        pre_buf[slot] = lax.dot_general(
            inputs_t[channels:, :],
            weights[channels:time_end, cols],
            LEFT_TRANSPOSED,
            preferred_element_type=F32,
        )
        in_buf[slot] = lax.dot_general(
            inputs_t[0:channels, :],
            weights[0:channels, cols],
            LEFT_TRANSPOSED,
            preferred_element_type=F32,
        )
        for start in range(0, rows_here, ROW_CHUNK):
            rows = pl.ds(start, ROW_CHUNK)
            half_pre = pre_buf[slot, rows, :]
            wave = jnp.tanh(half_pre)
            above = wave + 1.0
            silu = half_pre * above
            hidden = in_buf[slot, rows, :] + silu
            hid[rows, cols] = hidden.astype(BF16)
            slope[rows, cols] = (above + silu * (1.0 - wave)).astype(BF16)
            power = hidden * hidden
            partial = power[:, 0:LANES]
            for lane in range(LANES, FWD_COLUMNS, LANES):
                partial = partial + power[:, lane : lane + LANES]
            square[rows, :] += partial
    out_weight = weights[time_end:, :]
    scaled = (out_weight.astype(F32) * factor[0:1, :]).astype(BF16)
    out = lax.dot_general(hid[...], scaled, RIGHT_TRANSPOSED, preferred_element_type=F32)
    wide = jnp.broadcast_to(shift[0:1, :], (SHIFT_ROWS, shift.shape[1]))
    high = wide.astype(BF16).astype(F32)
    row = lax.broadcasted_iota(jnp.int32, wide.shape, 0)
    terms = jnp.where(row == 0, high, jnp.where(row == 1, wide - high, 0.0)).astype(BF16)
    bias = lax.dot_general(terms, out_weight, RIGHT_TRANSPOSED, preferred_element_type=F32)
    power = jnp.sum(square[...], axis=1, keepdims=True)
    stats[0:rows_here, :] = jnp.concatenate(
        [out, jnp.broadcast_to(power, (rows_here, LANES - channels))], axis=1
    )
    stats[rows_here:, :] = jnp.concatenate([bias, jnp.zeros_like(bias)], axis=1)


def forward(inputs_t, weights, factor, shift):
    rows, columns = inputs_t.shape[1], weights.shape[1]
    outs = [((rows, columns), BF16)] * 2 + [((rows + SHIFT_ROWS, LANES), F32)]
    scratch = [pltpu.VMEM((2, rows, FWD_COLUMNS), F32)] * 2 + [pltpu.VMEM((rows, LANES), F32)]
    flops = 2 * rows * columns * weights.shape[0]
    args = (inputs_t, weights, factor, shift)
    return local_call(forward_kernel, "forward", args, outs, scratch, flops=flops)


def make_backward_kernel(model_width, total_rows, added):
    def backward_kernel(
        own, got, target_t, hid, slope, weights, factor, shift, inputs_t, *rest
    ):
        before = rest[0] if added else None
        out, mod_buf, hid_buf, pre_buf, pull = rest[1:] if added else rest
        root = 1.0 / math.sqrt(model_width)
        channels, rows_here = target_t.shape
        time_end = inputs_t.shape[0]
        columns = out.shape[1]

        both = own[0:rows_here, :] + got[0:rows_here, :]
        raw = both[:, 0:channels]
        inverse = lax.rsqrt(both[:, channels : channels + 1] * (1.0 / model_width) + NORM_EPS)
        terms = own[rows_here:, 0:channels] + got[rows_here:, 0:channels]
        bias = jnp.sum(terms, axis=0, keepdims=True)
        output = (inverse * raw + bias) * root
        out_grad = (2.0 / (total_rows * channels)) * (output - target_t[...].T)
        grad = (out_grad * (inverse * root)).astype(BF16)
        wide = grad.astype(F32)
        grad_t = wide.T.astype(BF16)
        pulled = inverse * inverse * (1.0 / model_width)
        pulled = pulled * jnp.sum(wide * raw, axis=1, keepdims=True)
        pull[...] = jnp.broadcast_to(pulled, pull.shape)
        grad_sum = jnp.sum(out_grad.T, axis=1, keepdims=True) * root

        scaled = (weights[time_end:, :].astype(F32) * factor[0:1, :]).astype(BF16)
        mod_buf[...] = jnp.dot(grad, scaled, preferred_element_type=F32)
        for start in range(0, rows_here, ROW_CHUNK):
            rows = pl.ds(start, ROW_CHUNK)
            spread = jnp.concatenate([pull[rows, :]] * (columns // LANES), axis=1)
            hid_grad = mod_buf[rows, :] - hid[rows, :].astype(F32) * spread
            hid_buf[rows, :] = hid_grad.astype(BF16)
            pre_buf[rows, :] = (hid_grad * slope[rows, :].astype(F32)).astype(BF16)

        def put(rows, values):
            if added:
                values = values + before[rows, :]
            out[rows, :] = values.astype(out.dtype)

        put(
            slice(0, channels),
            jnp.dot(inputs_t[0:channels, :], hid_buf[...], preferred_element_type=F32),
        )
        put(
            slice(channels, time_end),
            jnp.dot(inputs_t[channels:, :], pre_buf[...], preferred_element_type=F32),
        )
        grad_out = jnp.dot(grad_t, hid[...], preferred_element_type=F32)
        put(
            slice(time_end, out.shape[0]),
            grad_out * factor[0:1, :] + grad_sum * shift[0:1, :],
        )

    return backward_kernel


def backward(stats, target_t, state, weights, factor, shift, inputs_t, before, sizes):
    rows, columns = state[0].shape
    scratch = [
        pltpu.VMEM((rows, columns), F32),
        pltpu.VMEM((rows, columns), BF16),
        pltpu.VMEM((rows, columns), BF16),
        pltpu.VMEM((rows, LANES), F32),
    ]
    flops = 2 * rows * columns * (weights.shape[0] + target_t.shape[0])
    args = (*stats, target_t, *state, weights, factor, shift, inputs_t, *before)
    outs = [(weights.shape, BF16 if before else F32)]
    kernel = make_backward_kernel(*sizes, bool(before))
    return local_call(kernel, "backward", args, outs, scratch, flops=flops)[0]


def prepare_kernel(
    core, latents, latents_got, noise, noise_got, levels, levels_got, modulation, *rest
):
    outs, (latent_buf, noise_buf, level_buf) = rest[:-3], rest[-3:]
    steps, channels, tokens = latents.shape
    half_width = (outs[0].shape[0] - channels) // 2
    pairs = ((latents, latents_got), (noise, noise_got), (levels, levels_got))
    for buffer, (own, got) in zip((latent_buf, noise_buf, level_buf), pairs):

        @pl.when(core[0] == 0)
        def _():
            buffer[0] = own[...]
            buffer[1] = got[...]

        @pl.when(core[0] != 0)
        def _():
            buffer[0] = got[...]
            buffer[1] = own[...]

    place = 0
    for step in range(steps):
        for owner in range(CORES):
            inputs_t, target_t = outs[place : place + 2]
            place += 2
            level = (level_buf[owner, step : step + 1, :].astype(F32) + 0.5) / LEVELS
            latent = latent_buf[owner, step].astype(F32)
            draw = noise_buf[owner, step].astype(F32)
            noised = ((1.0 - level) * latent + level * draw).astype(BF16).astype(F32)
            noised = noised * (1.0 / math.sqrt(channels))
            inputs_t[0:channels, :] = noised.astype(BF16)
            target_t[...] = draw - latent
            order = lax.broadcasted_iota(jnp.int32, (half_width, tokens), 0).astype(F32)
            angles = (1000.0 * level) * jnp.exp(-math.log(10000.0) * order / half_width)
            root = 0.5 / math.sqrt(2 * half_width)
            for part, wave in enumerate((jnp.cos(angles), jnp.sin(angles))):
                wave = wave.astype(BF16).astype(F32) * root
                inputs_t[pl.ds(channels + part * half_width, half_width), :] = wave.astype(BF16)
    rows = modulation[...]
    half = rows.shape[1] // CORES
    factor, shift = outs[place:]

    for side in range(CORES):

        @pl.when(core[0] == side)
        def _():
            here = rows[:, side * half : (side + 1) * half]
            factor[...] = 1.0 + here[1:2]
            shift[...] = here[0:1]


def prepare(core, latents, noise_draw, timesteps, mod_rows, time_width, width):
    steps, tokens, channels = latents.shape
    half = mod_rows.shape[1] // CORES
    outs = [
        ((channels + time_width, tokens), BF16),
        ((channels, tokens), F32),
    ] * (steps * CORES) + [((1, half), F32)] * 2
    args = []
    scratch = []
    for values in (latents.transpose(0, 2, 1), noise_draw.transpose(0, 2, 1), timesteps):
        args += [values, core_swap(values, width)]
        scratch.append(pltpu.VMEM((CORES,) + values.shape, values.dtype))
    results = local_call(
        prepare_kernel,
        "prepare",
        (*args, mod_rows),
        outs,
        scratch,
        scalars=(core,),
        flops=2**32,
    )
    sets = [results[2 * i : 2 * i + 2] for i in range(steps * CORES)]
    return [sets[CORES * s : CORES * (s + 1)] for s in range(steps)], results[-2:]


def adam(blocks, params, mean, square):
    halves = []
    for core in range(CORES):
        total = blocks[core].astype(F32)
        for index in range(core + CORES, blocks.shape[0], CORES):
            total = total + blocks[index].astype(F32)
        halves.append(total)
    gradient = jnp.concatenate(halves, axis=1)
    old = params[...]
    first = BETA_ONE * mean[...] + (1.0 - BETA_ONE) * gradient
    second = BETA_TWO * square[...] + (1.0 - BETA_TWO) * gradient * gradient
    new = old - INNER_RATE * (first / (jnp.sqrt(second) + ADAM_EPS) + DECAY_RATE * old)
    return first, second, new


def step_kernel(blocks, params, mean, square, new_mean, new_square, new_params, copies):
    first, second, new = adam(blocks, params, mean, square)
    new_mean[...] = first
    new_square[...] = second
    new_params[...] = new
    spread_halves(new, copies)


def last_kernel(blocks, params, mean, square, start, new_mean, new_square, *drifts):
    first, second, new = adam(blocks, params, mean, square)
    new_mean[...] = first
    new_square[...] = second
    drift = (start[...] - new).astype(BF16)
    for index, part in enumerate(drifts):
        columns = part.shape[1]
        part[...] = drift[:, index * columns : (index + 1) * columns]


def pair_add_kernel(mine, got, out):
    out[...] = (mine[...].astype(F32) + got[...].astype(F32)).astype(BF16)


def replica_sum(parts, replicas):
    bits = [1 << stage for stage in range(replicas.bit_length() - 1)]
    middle = len(bits) // 2
    parts = list(parts)
    for stage in zip(bits, bits[middle:] + bits[:middle]):
        got = [
            lax.ppermute(part, "replica", [(i, i ^ bit) for i in range(replicas)])
            for part, bit in zip(parts, stage)
        ]
        parts = [
            local_call(pair_add_kernel, "pair_add", pair, [(pair[0].shape, BF16)])[0]
            for pair in zip(parts, got)
        ]
    return parts


def make_outer_kernel(replicas):
    def outer_kernel(
        left, right, params, momentum, mean, square, new_params, new_momentum, *moments
    ):
        moments[0][...] = mean[...]
        moments[1][...] = square[...]
        for index, part in enumerate((left, right)):
            columns = part.shape[1]
            cols = slice(index * columns, (index + 1) * columns)
            average = part[...].astype(F32) * (1.0 / replicas)
            moved = NESTEROV * momentum[:, cols] + average
            new_momentum[:, cols] = moved
            new_params[:, cols] = params[:, cols] - OUTER_RATE * (average + NESTEROV * moved)

    return outer_kernel


def on_device(
    outer_params,
    outer_momentum,
    inner_mean,
    inner_square,
    latents,
    noise_draw,
    timesteps,
    fragment,
    modulation,
):
    width = lax.axis_size("fsdp")
    replicas = lax.axis_size("replica")
    core = (lax.axis_index("fsdp") % CORES).astype(jnp.int32).reshape(1)
    rows, model_width = outer_params.shape
    half = model_width // CORES
    channels = latents.shape[2]
    time_width = rows * width - 2 * channels
    total_rows = latents.shape[1] * width
    blocks_shape = (width, rows, half)

    gathered = exchange(spread_start(outer_params, width), "fsdp")
    mod_rows = lax.dynamic_index_in_dim(modulation, fragment[0], 0, keepdims=False)
    prepared, mods = prepare(
        core, latents, noise_draw, timesteps, mod_rows, time_width, width
    )
    gathered, prepared, mods = lax.optimization_barrier((gathered, prepared, mods))

    params, mean, square = outer_params, inner_mean[0], inner_square[0]
    sizes = (model_width, total_rows)
    factor, shift = mods
    moments = [(params.shape, F32)] * 2
    for step in range(STEPS):
        weights = gathered.reshape(width * rows, half)
        states = []
        for inputs_t, _ in prepared[step]:
            hid, slope, stats = forward(inputs_t, weights, factor, shift)
            states.append(((hid, slope), (stats, core_swap(stats, width))))
        gradient = ()
        for (state, stats), (inputs_t, target_t) in zip(states, prepared[step]):
            gradient = (
                backward(
                    stats, target_t, state, weights, factor, shift, inputs_t, gradient, sizes
                ),
            )
        blocks = exchange(gradient[0].reshape(blocks_shape), "fsdp")
        if step + 1 < STEPS:
            mean, square, params, copies = local_call(
                step_kernel,
                "update",
                (blocks, params, mean, square),
                moments + [(params.shape, F32), (blocks_shape, BF16)],
            )
            gathered = exchange(copies, "fsdp")
        else:
            mean, square, *drifts = local_call(
                last_kernel,
                "update_last",
                (blocks, params, mean, square, outer_params),
                moments + [((rows, half), BF16)] * 2,
            )
    drifts = replica_sum(drifts, replicas)
    new_params, new_momentum, mean, square = local_call(
        make_outer_kernel(replicas),
        "outer",
        (*drifts, outer_params, outer_momentum, mean, square),
        [(params.shape, F32)] * 4,
        hbm_outs=True,
    )
    return (new_params, new_momentum, mean[None], square[None])


def solution(mesh):
    return jax.shard_map(
        on_device,
        mesh=mesh,
        in_specs=(
            P("fsdp", None),
            P("fsdp", None),
            P("replica", "fsdp", None),
            P("replica", "fsdp", None),
            P(None, ("replica", "fsdp"), None),
            P(None, ("replica", "fsdp"), None),
            P(None, ("replica", "fsdp")),
            P(),
            P(),
        ),
        out_specs=(
            P("fsdp", None),
            P("fsdp", None),
            P("replica", "fsdp", None),
            P("replica", "fsdp", None),
        ),
        check_vma=False,
    )
```

```python
import math

import jax
import jax.numpy as jnp
from jax import lax
from jax.experimental import pallas as pl
from jax.experimental.pallas import tpu as pltpu
from jax.sharding import PartitionSpec as P

STEPS = 2
LEVELS = 1000


BETA_ONE = 0.9
BETA_TWO = 0.95
INNER_RATE = 0.2
DECAY_RATE = 0.1
ADAM_EPS = 1e-08
NORM_EPS = 1e-06
OUTER_RATE = 0.7
NESTEROV = 0.9

CORES = 2
LANES = 128
ROW_CHUNK = 16
FWD_COLUMNS = 256
BACK_COLUMNS = 512
START_PARTS = 2
KERNEL_VMEM = 24 * 2**20

BF16 = jnp.bfloat16
F32 = jnp.float32
VMEM = pl.BlockSpec(memory_space=pltpu.VMEM)
SMEM = pl.BlockSpec(memory_space=pltpu.SMEM)
RIGHT_TRANSPOSED = (((1,), (1,)), ((), ()))
LEFT_TRANSPOSED = (((0,), (0,)), ((), ()))
SHIFT_ROWS = 16


def local_call(kernel, name, args, outs, scratch=(), scalars=(), flops=0, hbm_outs=False):
    place = pltpu.VMEM if not hbm_outs else jax.ShapeDtypeStruct
    specs = [SMEM] * len(scalars) + [VMEM] * len(args)
    values = [*scalars, *(pltpu.with_memory_space_constraint(a, pltpu.VMEM) for a in args)]
    moved = sum(math.prod(o[0]) * 4 for o in outs) + sum(a.size * a.dtype.itemsize for a in args)
    return pl.pallas_call(
        kernel,
        in_specs=specs,
        out_specs=[VMEM] * len(outs),
        out_shape=[place(shape, dtype) for shape, dtype in outs],
        scratch_shapes=list(scratch),
        compiler_params=pltpu.CompilerParams(vmem_limit_bytes=KERNEL_VMEM),
        cost_estimate=pl.CostEstimate(flops=flops, bytes_accessed=moved, transcendentals=0),
        name=name,
    )(*values)


def core_swap(values, width):
    return lax.ppermute(values, "fsdp", [(i, i ^ 1) for i in range(width)])


def exchange(blocks, axis):
    return lax.all_to_all(blocks, axis, 0, 0)


def spread_halves(values, copies):
    half = values.shape[1] // CORES
    for core in range(CORES):
        block = values[:, core * half : (core + 1) * half].astype(BF16)
        for index in range(core, copies.shape[0], CORES):
            copies[index] = block


def start_kernel(params, copies):
    block = params[...].astype(BF16)
    for index in range(copies.shape[0]):
        copies[index, 0] = block


def spread_start(params, width):
    rows, columns = params.shape
    half = columns // CORES
    part = half // START_PARTS
    shape = (width // CORES, CORES, rows, half)
    copies = pl.pallas_call(
        start_kernel,
        grid=(CORES, START_PARTS),
        in_specs=[
            pl.BlockSpec((rows, part), lambda core, place: (0, core * START_PARTS + place))
        ],
        out_specs=pl.BlockSpec(
            (shape[0], 1, rows, part), lambda core, place: (0, core, 0, place)
        ),
        out_shape=jax.ShapeDtypeStruct(shape, BF16),
        compiler_params=pltpu.CompilerParams(vmem_limit_bytes=KERNEL_VMEM),
        name="start",
    )(pltpu.with_memory_space_constraint(params, pltpu.HBM))
    return copies.reshape(width, rows, half)


def forward_kernel(inputs_t, weights, factor, shift, hid, slope, stats, pre_buf, in_buf, square):
    time_end, rows_here = inputs_t.shape
    channels = weights.shape[0] - time_end
    square[...] = jnp.zeros_like(square)
    for index in range(weights.shape[1] // FWD_COLUMNS):
        slot = index % 2
        cols = pl.ds(index * FWD_COLUMNS, FWD_COLUMNS)
        pre_buf[slot] = lax.dot_general(
            inputs_t[channels:, :],
            weights[channels:time_end, cols],
            LEFT_TRANSPOSED,
            preferred_element_type=F32,
        )
        in_buf[slot] = lax.dot_general(
            inputs_t[0:channels, :],
            weights[0:channels, cols],
            LEFT_TRANSPOSED,
            preferred_element_type=F32,
        )
        for start in range(0, rows_here, ROW_CHUNK):
            rows = pl.ds(start, ROW_CHUNK)
            half_pre = pre_buf[slot, rows, :]
            wave = jnp.tanh(half_pre)
            above = wave + 1.0
            silu = half_pre * above
            hidden = in_buf[slot, rows, :] + silu
            hid[rows, cols] = hidden.astype(BF16)
            slope[rows, cols] = (above + silu * (1.0 - wave)).astype(BF16)
            power = hidden * hidden
            partial = power[:, 0:LANES]
            for lane in range(LANES, FWD_COLUMNS, LANES):
                partial = partial + power[:, lane : lane + LANES]
            square[rows, :] += partial
    out_weight = weights[time_end:, :]
    scaled = (out_weight.astype(F32) * factor[0:1, :]).astype(BF16)
    out = lax.dot_general(hid[...], scaled, RIGHT_TRANSPOSED, preferred_element_type=F32)
    wide = jnp.broadcast_to(shift[0:1, :], (SHIFT_ROWS, shift.shape[1]))
    high = wide.astype(BF16).astype(F32)
    row = lax.broadcasted_iota(jnp.int32, wide.shape, 0)
    terms = jnp.where(row == 0, high, jnp.where(row == 1, wide - high, 0.0)).astype(BF16)
    bias = lax.dot_general(terms, out_weight, RIGHT_TRANSPOSED, preferred_element_type=F32)
    power = jnp.sum(square[...], axis=1, keepdims=True)
    stats[0:rows_here, :] = jnp.concatenate(
        [out, jnp.broadcast_to(power, (rows_here, LANES - channels))], axis=1
    )
    stats[rows_here:, :] = jnp.concatenate([bias, jnp.zeros_like(bias)], axis=1)


def forward(inputs_t, weights, factor, shift):
    rows, columns = inputs_t.shape[1], weights.shape[1]
    outs = [((rows, columns), BF16)] * 2 + [((rows + SHIFT_ROWS, LANES), F32)]
    scratch = [pltpu.VMEM((2, rows, FWD_COLUMNS), F32)] * 2 + [pltpu.VMEM((rows, LANES), F32)]
    flops = 2 * rows * columns * weights.shape[0]
    args = (inputs_t, weights, factor, shift)
    return local_call(forward_kernel, "forward", args, outs, scratch, flops=flops)


def make_backward_kernel(model_width, total_rows, added):
    def backward_kernel(
        own, got, target_t, hid, slope, weights, factor, shift, inputs_t, *rest
    ):
        before = rest[0] if added else None
        out, mod_buf, hid_buf, pre_buf, pull = rest[1:] if added else rest
        root = 1.0 / math.sqrt(model_width)
        channels, rows_here = target_t.shape
        time_end = inputs_t.shape[0]
        columns = out.shape[1]

        both = own[0:rows_here, :] + got[0:rows_here, :]
        raw = both[:, 0:channels]
        inverse = lax.rsqrt(both[:, channels : channels + 1] * (1.0 / model_width) + NORM_EPS)
        terms = own[rows_here:, 0:channels] + got[rows_here:, 0:channels]
        bias = jnp.sum(terms, axis=0, keepdims=True)
        output = (inverse * raw + bias) * root
        out_grad = (2.0 / (total_rows * channels)) * (output - target_t[...].T)
        grad = (out_grad * (inverse * root)).astype(BF16)
        wide = grad.astype(F32)
        grad_t = wide.T.astype(BF16)
        pulled = inverse * inverse * (1.0 / model_width)
        pulled = pulled * jnp.sum(wide * raw, axis=1, keepdims=True)
        pull[...] = jnp.broadcast_to(pulled, pull.shape)
        grad_sum = jnp.sum(out_grad.T, axis=1, keepdims=True) * root

        scaled = (weights[time_end:, :].astype(F32) * factor[0:1, :]).astype(BF16)
        for left in range(0, columns, BACK_COLUMNS):
            cols = pl.ds(left, BACK_COLUMNS)
            mod_buf[:, cols] = jnp.dot(
                grad, scaled[:, left : left + BACK_COLUMNS], preferred_element_type=F32
            )
            for start in range(0, rows_here, ROW_CHUNK):
                rows = pl.ds(start, ROW_CHUNK)
                spread = jnp.concatenate([pull[rows, :]] * (BACK_COLUMNS // LANES), axis=1)
                hid_grad = mod_buf[rows, cols] - hid[rows, cols].astype(F32) * spread
                hid_buf[rows, cols] = hid_grad.astype(BF16)
                pre_buf[rows, cols] = (hid_grad * slope[rows, cols].astype(F32)).astype(BF16)

        def put(rows, values):
            if added:
                values = values + before[rows, :]
            out[rows, :] = values.astype(out.dtype)

        put(
            slice(0, channels),
            jnp.dot(inputs_t[0:channels, :], hid_buf[...], preferred_element_type=F32),
        )
        put(
            slice(channels, time_end),
            jnp.dot(inputs_t[channels:, :], pre_buf[...], preferred_element_type=F32),
        )
        grad_out = jnp.dot(grad_t, hid[...], preferred_element_type=F32)
        put(
            slice(time_end, out.shape[0]),
            grad_out * factor[0:1, :] + grad_sum * shift[0:1, :],
        )

    return backward_kernel


def backward(stats, target_t, state, weights, factor, shift, inputs_t, before, sizes):
    rows, columns = state[0].shape
    scratch = [
        pltpu.VMEM((rows, columns), F32),
        pltpu.VMEM((rows, columns), BF16),
        pltpu.VMEM((rows, columns), BF16),
        pltpu.VMEM((rows, LANES), F32),
    ]
    flops = 2 * rows * columns * (weights.shape[0] + target_t.shape[0])
    args = (*stats, target_t, *state, weights, factor, shift, inputs_t, *before)
    outs = [(weights.shape, BF16 if before else F32)]
    kernel = make_backward_kernel(*sizes, bool(before))
    return local_call(kernel, "backward", args, outs, scratch, flops=flops)[0]


def prepare_kernel(
    core, latents, latents_got, noise, noise_got, levels, levels_got, modulation, *rest
):
    outs, (latent_buf, noise_buf, level_buf) = rest[:-3], rest[-3:]
    steps, channels, tokens = latents.shape
    half_width = (outs[0].shape[0] - channels) // 2
    pairs = ((latents, latents_got), (noise, noise_got), (levels, levels_got))
    for buffer, (own, got) in zip((latent_buf, noise_buf, level_buf), pairs):

        @pl.when(core[0] == 0)
        def _():
            buffer[0] = own[...]
            buffer[1] = got[...]

        @pl.when(core[0] != 0)
        def _():
            buffer[0] = got[...]
            buffer[1] = own[...]

    place = 0
    for step in range(steps):
        for owner in range(CORES):
            inputs_t, target_t = outs[place : place + 2]
            place += 2
            level = (level_buf[owner, step : step + 1, :].astype(F32) + 0.5) / LEVELS
            latent = latent_buf[owner, step].astype(F32)
            draw = noise_buf[owner, step].astype(F32)
            noised = ((1.0 - level) * latent + level * draw).astype(BF16).astype(F32)
            noised = noised * (1.0 / math.sqrt(channels))
            inputs_t[0:channels, :] = noised.astype(BF16)
            target_t[...] = draw - latent
            order = lax.broadcasted_iota(jnp.int32, (half_width, tokens), 0).astype(F32)
            angles = (1000.0 * level) * jnp.exp(-math.log(10000.0) * order / half_width)
            root = 0.5 / math.sqrt(2 * half_width)
            for part, wave in enumerate((jnp.cos(angles), jnp.sin(angles))):
                wave = wave.astype(BF16).astype(F32) * root
                inputs_t[pl.ds(channels + part * half_width, half_width), :] = wave.astype(BF16)
    rows = modulation[...]
    half = rows.shape[1] // CORES
    factor, shift = outs[place:]

    for side in range(CORES):

        @pl.when(core[0] == side)
        def _():
            here = rows[:, side * half : (side + 1) * half]
            factor[...] = 1.0 + here[1:2]
            shift[...] = here[0:1]


def prepare(core, latents, noise_draw, timesteps, mod_rows, time_width, width):
    steps, tokens, channels = latents.shape
    half = mod_rows.shape[1] // CORES
    outs = [
        ((channels + time_width, tokens), BF16),
        ((channels, tokens), F32),
    ] * (steps * CORES) + [((1, half), F32)] * 2
    args = []
    scratch = []
    for values in (latents.transpose(0, 2, 1), noise_draw.transpose(0, 2, 1), timesteps):
        args += [values, core_swap(values, width)]
        scratch.append(pltpu.VMEM((CORES,) + values.shape, values.dtype))
    results = local_call(
        prepare_kernel,
        "prepare",
        (*args, mod_rows),
        outs,
        scratch,
        scalars=(core,),
        flops=2**32,
    )
    sets = [results[2 * i : 2 * i + 2] for i in range(steps * CORES)]
    return [sets[CORES * s : CORES * (s + 1)] for s in range(steps)], results[-2:]


def adam(blocks, params, mean, square):
    halves = []
    for core in range(CORES):
        total = blocks[core].astype(F32)
        for index in range(core + CORES, blocks.shape[0], CORES):
            total = total + blocks[index].astype(F32)
        halves.append(total)
    gradient = jnp.concatenate(halves, axis=1)
    old = params[...]
    first = BETA_ONE * mean[...] + (1.0 - BETA_ONE) * gradient
    second = BETA_TWO * square[...] + (1.0 - BETA_TWO) * gradient * gradient
    new = old - INNER_RATE * (first / (jnp.sqrt(second) + ADAM_EPS) + DECAY_RATE * old)
    return first, second, new


def step_kernel(blocks, params, mean, square, new_mean, new_square, new_params, copies):
    first, second, new = adam(blocks, params, mean, square)
    new_mean[...] = first
    new_square[...] = second
    new_params[...] = new
    spread_halves(new, copies)


def last_kernel(blocks, params, mean, square, start, new_mean, new_square, *drifts):
    first, second, new = adam(blocks, params, mean, square)
    new_mean[...] = first
    new_square[...] = second
    drift = (start[...] - new).astype(BF16)
    for index, part in enumerate(drifts):
        columns = part.shape[1]
        part[...] = drift[:, index * columns : (index + 1) * columns]


def pair_add_kernel(mine, got, out):
    out[...] = (mine[...].astype(F32) + got[...].astype(F32)).astype(BF16)


def replica_sum(parts, replicas):
    bits = [1 << stage for stage in range(replicas.bit_length() - 1)]
    middle = len(bits) // 2
    parts = list(parts)
    for stage in zip(bits, bits[middle:] + bits[:middle]):
        got = [
            lax.ppermute(part, "replica", [(i, i ^ bit) for i in range(replicas)])
            for part, bit in zip(parts, stage)
        ]
        parts = [
            local_call(pair_add_kernel, "pair_add", pair, [(pair[0].shape, BF16)])[0]
            for pair in zip(parts, got)
        ]
    return parts


def make_outer_kernel(replicas):
    def outer_kernel(
        left, right, params, momentum, mean, square, new_params, new_momentum, *moments
    ):
        moments[0][...] = mean[...]
        moments[1][...] = square[...]
        for index, part in enumerate((left, right)):
            columns = part.shape[1]
            cols = slice(index * columns, (index + 1) * columns)
            average = part[...].astype(F32) * (1.0 / replicas)
            moved = NESTEROV * momentum[:, cols] + average
            new_momentum[:, cols] = moved
            new_params[:, cols] = params[:, cols] - OUTER_RATE * (average + NESTEROV * moved)

    return outer_kernel


def on_device(
    outer_params,
    outer_momentum,
    inner_mean,
    inner_square,
    latents,
    noise_draw,
    timesteps,
    fragment,
    modulation,
):
    width = lax.axis_size("fsdp")
    replicas = lax.axis_size("replica")
    core = (lax.axis_index("fsdp") % CORES).astype(jnp.int32).reshape(1)
    rows, model_width = outer_params.shape
    half = model_width // CORES
    channels = latents.shape[2]
    time_width = rows * width - 2 * channels
    total_rows = latents.shape[1] * width
    blocks_shape = (width, rows, half)

    gathered = exchange(spread_start(outer_params, width), "fsdp")
    mod_rows = lax.dynamic_index_in_dim(modulation, fragment[0], 0, keepdims=False)
    prepared, mods = prepare(
        core, latents, noise_draw, timesteps, mod_rows, time_width, width
    )
    gathered, prepared, mods = lax.optimization_barrier((gathered, prepared, mods))

    params, mean, square = outer_params, inner_mean[0], inner_square[0]
    sizes = (model_width, total_rows)
    factor, shift = mods
    moments = [(params.shape, F32)] * 2
    for step in range(STEPS):
        weights = gathered.reshape(width * rows, half)
        states = []
        for inputs_t, _ in prepared[step]:
            hid, slope, stats = forward(inputs_t, weights, factor, shift)
            states.append(((hid, slope), (stats, core_swap(stats, width))))
        gradient = ()
        for (state, stats), (inputs_t, target_t) in zip(states, prepared[step]):
            gradient = (
                backward(
                    stats, target_t, state, weights, factor, shift, inputs_t, gradient, sizes
                ),
            )
        blocks = exchange(gradient[0].reshape(blocks_shape), "fsdp")
        if step + 1 < STEPS:
            mean, square, params, copies = local_call(
                step_kernel,
                "update",
                (blocks, params, mean, square),
                moments + [(params.shape, F32), (blocks_shape, BF16)],
            )
            gathered = exchange(copies, "fsdp")
        else:
            mean, square, *drifts = local_call(
                last_kernel,
                "update_last",
                (blocks, params, mean, square, outer_params),
                moments + [((rows, half), BF16)] * 2,
            )
    drifts = replica_sum(drifts, replicas)
    new_params, new_momentum, mean, square = local_call(
        make_outer_kernel(replicas),
        "outer",
        (*drifts, outer_params, outer_momentum, mean, square),
        [(params.shape, F32)] * 4,
        hbm_outs=True,
    )
    return (new_params, new_momentum, mean[None], square[None])


def solution(mesh):
    return jax.shard_map(
        on_device,
        mesh=mesh,
        in_specs=(
            P("fsdp", None),
            P("fsdp", None),
            P("replica", "fsdp", None),
            P("replica", "fsdp", None),
            P(None, ("replica", "fsdp"), None),
            P(None, ("replica", "fsdp"), None),
            P(None, ("replica", "fsdp")),
            P(),
            P(),
        ),
        out_specs=(
            P("fsdp", None),
            P("fsdp", None),
            P("replica", "fsdp", None),
            P("replica", "fsdp", None),
        ),
        check_vma=False,
    )
```
